32 devices in a mesh: ctx: 8 (over y, x, core), head: 4 (over z).
Axes of the slice: x: 2, y: 2, z: 4, core: 2. Of those that a mesh axis runs over, the one named last changes fastest.
Arguments:
- query_in: bfloat16 [1024, 1024], P(('ctx', 'head')), may hold values from -20 to 20
- key_in: bfloat16 [1024, 1024], P('ctx', 'head'), may hold values from -20 to 20
- value_in: bfloat16 [1024, 1024], P('ctx', 'head'), may hold values from -6 to 6
- out_saved: bfloat16 [1024, 1024], P(('ctx', 'head')), may hold values from -1.5 to 1.5
- out_grad: bfloat16 [1024, 1024], P(('ctx', 'head')), may hold values from -24 to 24
- span_place: int32 [16], replicated, may hold values from 0 to 15, each once
Outputs:
- grad_query: bfloat16 [1024, 1024], P(('ctx', 'head'))
- grad_key: bfloat16 [1024, 1024], P('ctx', 'head')
- grad_value: bfloat16 [1024, 1024], P('ctx', 'head')
The draws below stay inside these ranges and needn't reach their ends.
Inputs may be any that keep to these rules, and one draw needn't show every extreme that they name: `span_place`: each block position appears once.
All inputs are finite; a program needn't handle non-finite values.
Results may differ from the reference program's by a relative error of at most 0.0049.
Values may be sent and summed in bfloat16 or wider, within the bound.
A program may use at most 64 MiB of HBM per device.

```python
import jax
import jax.numpy as jnp
from jax import lax

HEAD_DIM = 128
HEADS = 8
SPAN = 64
SPANS = 16
SEQUENCE_TOKENS = 1024


def drawn_pair(key):
    root_random_key = jax.random.fold_in(key, 4242)
    random_key_for_queries, random_key_for_keys = jax.random.split(root_random_key, 2)
    shape = (SEQUENCE_TOKENS, HEADS * HEAD_DIM)
    queries = jnp.clip(jax.random.normal(random_key_for_queries, shape, jnp.float32), -6.0, 6.0)
    keyset = jnp.clip(jax.random.normal(random_key_for_keys, shape, jnp.float32), -6.0, 6.0)
    return (queries, keyset)


def draw_query_in(key, part):
    return drawn_pair(key)[0].astype(jnp.bfloat16)


def draw_key_in(key, part):
    return drawn_pair(key)[1].astype(jnp.bfloat16)


def shard_levels(stream_key, dims, cuts, low, top_value):
    level, own = 1.0, jax.random.fold_in(stream_key, 6)
    for dim, blocks in cuts:
        heights = jnp.exp(jax.random.uniform(jax.random.fold_in(own, dim), (blocks,), jnp.float32, low / len(cuts), top_value / len(cuts)))
        level = level * jnp.repeat(heights, dims[dim] // blocks).reshape([-1 if axis == dim else 1 for axis in range(len(dims))])
    return level


def centred(rng, shape, width, bound, cuts=(), kind=jnp.bfloat16):
    entries = width * jax.random.normal(rng, shape, jnp.float32)
    if cuts:
        entries = entries * shard_levels(rng, shape, cuts, -0.22, 0.18)
    return jnp.clip(entries, -bound, bound).astype(kind)


def setup_inputs(seed: int = 0) -> dict:
    streams_of = jax.random.split(jax.random.key(seed), 7)
    query_in = draw_query_in(jax.random.fold_in(streams_of[6], 71), 0)
    key_in = draw_key_in(jax.random.fold_in(streams_of[6], 71), 0)
    value_in = centred(streams_of[2], (SEQUENCE_TOKENS, HEADS * HEAD_DIM), 1.0, 6.0, ((0, 8), (1, 4)))
    out_saved = centred(streams_of[3], (SEQUENCE_TOKENS, HEADS * HEAD_DIM), 0.25, 1.5, ((0, 32),))
    out_grad = centred(streams_of[4], (SEQUENCE_TOKENS, HEADS * HEAD_DIM), 4.0, 24.0, ((0, 32),))
    span_place = jax.random.permutation(streams_of[5], SPANS).astype(jnp.int32)
    return {"query_in": query_in, "key_in": key_in, "value_in": value_in, "out_saved": out_saved, "out_grad": out_grad, "span_place": span_place}


def reference(query_in, key_in, value_in, out_saved, out_grad, span_place):
    scale = HEAD_DIM ** -0.5
    index = jnp.arange(SEQUENCE_TOKENS, dtype=jnp.int32)
    position = span_place[index // SPAN].astype(jnp.int32) * SPAN + index % SPAN
    visible = position[None, :] <= position[:, None]

    def split_heads(array):
        return array.reshape(SEQUENCE_TOKENS, HEADS, HEAD_DIM).transpose(1, 0, 2)

    delta_all = jnp.sum((out_grad.astype(jnp.float32) * out_saved.astype(jnp.float32)).reshape(SEQUENCE_TOKENS, HEADS, HEAD_DIM), axis=2).T

    def one_head(operands):
        query_head, key_head, value_head, grad_head, delta_head = operands
        scores = jnp.dot(query_head, key_head.T, preferred_element_type=jnp.float32) * scale
        masked = jnp.where(visible, scores, -jnp.inf)
        top = jnp.max(masked, axis=1, keepdims=True)
        lse = top + jnp.log(jnp.sum(jnp.exp(masked - top), axis=1, keepdims=True))
        probs = jnp.exp(jnp.where(visible, scores - lse, -jnp.inf))
        dprobs = jnp.dot(grad_head, value_head.T, preferred_element_type=jnp.float32)
        dscores = (probs * (dprobs - delta_head[:, None]) * scale).astype(jnp.bfloat16)
        grad_q = jnp.dot(dscores, key_head, preferred_element_type=jnp.float32).astype(jnp.bfloat16)
        grad_k = jnp.dot(dscores.T, query_head, preferred_element_type=jnp.float32).astype(jnp.bfloat16)
        grad_v = jnp.dot(probs.astype(jnp.bfloat16).T, grad_head, preferred_element_type=jnp.float32).astype(jnp.bfloat16)
        return grad_q, grad_k, grad_v

    grads = lax.map(one_head, (split_heads(query_in), split_heads(key_in), split_heads(value_in), split_heads(out_grad), delta_all))

    def join_heads(array):
        return array.transpose(1, 0, 2).reshape(SEQUENCE_TOKENS, HEADS * HEAD_DIM)

    return join_heads(grads[0]), join_heads(grads[1]), join_heads(grads[2])
```

```python
import functools
import math

import jax
import jax.numpy as jnp
from jax import lax
from jax.experimental import pallas as pl
from jax.experimental.pallas import tpu as pltpu
from jax.sharding import PartitionSpec as P

HEAD_DIM = 128
CORES = 2
MESH = pl.DeviceIdType.MESH
NT = (((1,), (1,)), ((), ()))
NN = (((1,), (0,)), ((), ()))
TN = (((0,), (0,)), ((), ()))


def matmul(a, b, dims):
    return lax.dot_general(a, b, dims, preferred_element_type=jnp.float32)


def columns(index):
    return pl.ds(pl.multiple_of(index * HEAD_DIM, HEAD_DIM), HEAD_DIM)


def kernel(
    ctx_size, head_size, place, query_in, key_in, value_in, saved_in, grad_in,
    dq_out, dk_out, dv_out,
    qbuf, gbuf, dbuf, kbuf, vbuf, pbuf, dk_stage, dv_stage, dq_stage, kpart, vpart, qpart,
    own_grad, own_saved, delta_src,
    send_sem, local_sem, q_sem, g_sem, d_sem, k_sem, v_sem, kp_sem, vp_sem, qp_sem,
):
    chips = ctx_size // CORES
    rows_high = max(chips // 2, 1)
    block = key_in.shape[0]
    token_rows = query_in.shape[0]
    heads = head_size * CORES
    rows = CORES * block
    span = ctx_size * block // place.shape[0]
    spans = rows // span
    scale = HEAD_DIM ** -0.5

    me = lax.axis_index("ctx")
    z = lax.axis_index("head")
    core = lax.rem(me, CORES)
    chip = me // CORES
    low, high = lax.rem(chip, 2), chip // 2

    def other_chip(step):
        return lax.rem(high + step // 2, rows_high) * 2 + lax.rem(low + step % 2, 2)

    def other_core(step):
        return lax.rem(core + step, CORES)

    def other_z(step):
        return lax.rem(z + step, head_size)

    chip_at = [other_chip(step) for step in range(chips)]
    core_at = [other_core(step) for step in range(CORES)]
    z_at = [other_z(step) for step in range(head_size)]
    plane = [(c, j) for c in range(chips) for j in range(CORES) if c or j]
    line = [(w, j) for w in range(head_size) for j in range(CORES) if w or j]

    def plane_id(c, j):
        return {"ctx": chip_at[c] * CORES + core_at[j], "head": z}

    def line_id(w, j):
        return {"ctx": chip * CORES + core_at[j], "head": z_at[w]}

    barrier = pltpu.get_barrier_semaphore()
    peers = [plane_id(c, j) for c, j in plane] + [line_id(w, j) for w, j in line if w]
    for peer in peers:
        pl.semaphore_signal(barrier, inc=1, device_id=peer, device_id_type=MESH)

    grad_load = pltpu.make_async_copy(grad_in, own_grad, local_sem.at[0])
    saved_load = pltpu.make_async_copy(saved_in, own_saved, local_sem.at[1])
    grad_load.start()
    saved_load.start()
    my_head = z * CORES + core
    pltpu.make_async_copy(query_in.at[:, columns(my_head)], qbuf.at[core, z], q_sem.at[core, z]).start()
    pltpu.make_async_copy(key_in.at[:, columns(core)], kbuf.at[chip, core], k_sem.at[chip, core]).start()
    pltpu.make_async_copy(grad_in.at[:, columns(my_head)], gbuf.at[core, z], g_sem.at[core, z]).start()
    pltpu.make_async_copy(value_in.at[:, columns(core)], vbuf.at[chip, core], v_sem.at[chip, core]).start()

    grad_load.wait()
    saved_load.wait()
    product = own_grad[...].astype(jnp.float32) * own_saved[...].astype(jnp.float32)
    coarse = product.astype(jnp.bfloat16)
    fine = (product - coarse.astype(jnp.float32)).astype(jnp.bfloat16)
    shape = (heads, heads * HEAD_DIM)
    member = lax.broadcasted_iota(jnp.int32, shape, 1) // HEAD_DIM == lax.broadcasted_iota(jnp.int32, shape, 0)
    member = jnp.where(member, 1.0, 0.0).astype(jnp.bfloat16)
    delta = matmul(member, jnp.concatenate([coarse] * head_size, axis=0), NT)
    delta += matmul(member, jnp.concatenate([fine] * head_size, axis=0), NT)
    lane_z = lax.broadcasted_iota(jnp.int32, (heads, block), 1) // token_rows
    delta = jnp.where(lane_z == z, delta, 0.0)
    for h in range(heads):
        delta_src[h] = delta[h : h + 1]
    dbuf[core, z] = delta_src[my_head]

    pl.semaphore_wait(barrier, len(peers))

    sent = []

    def send(src, dst, sem, device):
        copy = pltpu.make_async_remote_copy(
            src_ref=src, dst_ref=dst, send_sem=send_sem.at[len(sent)], recv_sem=sem,
            device_id=device, device_id_type=MESH,
        )
        copy.start()
        sent.append(copy)

    def arrive(dst, sem):
        pltpu.make_async_copy(dst, dst, sem).wait()

    def send_plane(src, dst, sem):
        for c, j in plane[::-1]:
            send(src.at[:, columns(core_at[j])], dst.at[chip, core], sem.at[chip, core], plane_id(c, j))

    def send_line(src, dst, sem):
        for w, j in line:
            head = z_at[w] * CORES + core_at[j]
            send(src.at[:, columns(head)], dst.at[core, z], sem.at[core, z], line_id(w, j))

    send_line(query_in, qbuf, q_sem)
    send_plane(key_in, kbuf, k_sem)
    send_line(grad_in, gbuf, g_sem)
    send_plane(value_in, vbuf, v_sem)
    for w, j in line:
        head = z_at[w] * CORES + core_at[j]
        send(delta_src.at[head], dbuf.at[core, z], d_sem.at[core, z], line_id(w, j))

    lane = lax.broadcasted_iota(jnp.int32, (1, rows), 1)
    place_row = jnp.zeros((1, rows), jnp.int32)
    for s in range(spans):
        place_row = jnp.where(lane // span == s, place[chip * spans + s], place_row)
    pos_row = place_row * span + lane % span
    within = lax.broadcasted_iota(jnp.int32, (span, rows), 0)

    for j in range(CORES):
        for w in range(head_size):
            arrive(qbuf.at[j, w], q_sem.at[j, w])
    query = qbuf[...].reshape(rows, HEAD_DIM)

    tops, sums = [], []
    for c in range(chips):
        for j in range(CORES):
            arrive(kbuf.at[chip_at[c], j], k_sem.at[chip_at[c], j])
        keys = kbuf[chip_at[c]].reshape(rows, HEAD_DIM)
        scores = matmul(keys, query, NT) * (scale * math.log2(math.e))
        pieces = []
        for s in range(spans):
            limit = pos_row - place[chip_at[c] * spans + s] * span
            pieces.append(jnp.where(within <= limit, scores[s * span : (s + 1) * span], -1e30))
        masked = jnp.concatenate(pieces, axis=0)
        top = jnp.max(masked, axis=0, keepdims=True)
        probs = jnp.exp2(masked - top)
        pbuf[c] = probs
        tops.append(top)
        sums.append(jnp.sum(probs, axis=0, keepdims=True))

    best = functools.reduce(jnp.maximum, tops)
    weights = [jnp.exp2(top - best) for top in tops]
    total = functools.reduce(jnp.add, [w * s for w, s in zip(weights, sums)])
    weights = [w / total for w in weights]

    for j in range(CORES):
        for w in range(head_size):
            arrive(gbuf.at[j, w], g_sem.at[j, w])
    grad = gbuf[...].reshape(rows, HEAD_DIM)
    for w, j in line:
        arrive(dbuf.at[core_at[j], z_at[w]], d_sem.at[core_at[j], z_at[w]])
    delta_row = jnp.concatenate(
        [functools.reduce(jnp.add, [dbuf[j, w] for w in range(head_size)]) for j in range(CORES)], axis=1
    )

    grad_q = jnp.zeros((rows, HEAD_DIM), jnp.float32)
    for c in range(chips)[::-1]:
        for j in range(CORES):
            arrive(vbuf.at[chip_at[c], j], v_sem.at[chip_at[c], j])
        values = vbuf[chip_at[c]].reshape(rows, HEAD_DIM)
        probs = pbuf[c] * weights[c]
        dv_stage[c] = matmul(probs.astype(jnp.bfloat16), grad, NN).astype(jnp.bfloat16).reshape(dv_stage.shape[1:])
        dprobs = matmul(values, grad, NT)
        dscores = (probs * (dprobs - delta_row) * scale).astype(jnp.bfloat16)
        dk_stage[c] = matmul(dscores, query, NN).astype(jnp.bfloat16).reshape(dk_stage.shape[1:])
        for stage, part, sem in ((dv_stage, vpart, vp_sem), (dk_stage, kpart, kp_sem)):
            for j in range(CORES):
                if c or j:
                    send(stage.at[c, core_at[j]], part.at[chip, core], sem.at[chip, core], plane_id(c, j))
                else:
                    part[chip, core] = stage[c, core]
        grad_q += matmul(dscores, kbuf[chip_at[c]].reshape(rows, HEAD_DIM), TN)

    dq_stage[...] = grad_q.astype(jnp.bfloat16).reshape(dq_stage.shape)
    qpart[my_head] = dq_stage[core, z]
    for w, j in line:
        send(dq_stage.at[core_at[j], z_at[w]], qpart.at[my_head], qp_sem.at[my_head], line_id(w, j))

    for part, sem, out in ((vpart, vp_sem, dv_out), (kpart, kp_sem, dk_out)):
        for c, j in plane:
            arrive(part.at[chip_at[c], core_at[j]], sem.at[chip_at[c], core_at[j]])
        for j in range(CORES):
            summed = part[0, j].astype(jnp.float32)
            for c in range(1, chips):
                summed += part[c, j].astype(jnp.float32)
            out[:, j * HEAD_DIM : (j + 1) * HEAD_DIM] = summed.astype(jnp.bfloat16)

    for w, j in line:
        head = z_at[w] * CORES + core_at[j]
        arrive(qpart.at[head], qp_sem.at[head])
    for h in range(heads):
        dq_out[:, h * HEAD_DIM : (h + 1) * HEAD_DIM] = qpart[h]
    for copy in sent:
        copy.wait_send()


def body(query_in, key_in, value_in, out_saved, out_grad, span_place):
    ctx_size, head_size = lax.axis_size("ctx"), lax.axis_size("head")
    chips = ctx_size // CORES
    block = key_in.shape[0]
    token_rows, width = query_in.shape
    heads = head_size * CORES
    rows = CORES * block
    low = jnp.bfloat16
    tokens = (CORES, head_size, token_rows, HEAD_DIM)
    keys = (chips, CORES, block, HEAD_DIM)
    dma = pltpu.SemaphoreType.DMA
    copies = 4 * (ctx_size - 1) + 4 * (heads - 1)
    vmem = pl.BlockSpec(memory_space=pltpu.VMEM)
    hbm = pl.BlockSpec(memory_space=pl.ANY)
    smem = pl.BlockSpec(memory_space=pltpu.SMEM)
    pairs = CORES * chips * rows * rows
    return pl.pallas_call(
        functools.partial(kernel, ctx_size, head_size),
        out_shape=(
            jax.ShapeDtypeStruct(query_in.shape, low),
            jax.ShapeDtypeStruct(key_in.shape, low),
            jax.ShapeDtypeStruct(value_in.shape, low),
        ),
        in_specs=[smem] + [hbm] * 5,
        out_specs=(vmem, vmem, vmem),
        scratch_shapes=[
            pltpu.VMEM(tokens, low),
            pltpu.VMEM(tokens, low),
            pltpu.VMEM((CORES, head_size, 1, block), jnp.float32),
            pltpu.VMEM(keys, low),
            pltpu.VMEM(keys, low),
            pltpu.VMEM((chips, rows, rows), jnp.float32),
            pltpu.VMEM(keys, low),
            pltpu.VMEM(keys, low),
            pltpu.VMEM(tokens, low),
            pltpu.VMEM(keys, low),
            pltpu.VMEM(keys, low),
            pltpu.VMEM((heads, token_rows, HEAD_DIM), low),
            pltpu.VMEM((token_rows, width), low),
            pltpu.VMEM((token_rows, width), low),
            pltpu.VMEM((heads, 1, block), jnp.float32),
            dma((copies,)),
            dma((2,)),
            dma((CORES, head_size)),
            dma((CORES, head_size)),
            dma((CORES, head_size)),
            dma((chips, CORES)),
            dma((chips, CORES)),
            dma((chips, CORES)),
            dma((chips, CORES)),
            dma((heads,)),
        ],
        compiler_params=pltpu.CompilerParams(
            collective_id=0, has_side_effects=True, vmem_limit_bytes=40 * 1024 * 1024
        ),
        cost_estimate=pl.CostEstimate(
            flops=5 * pairs * HEAD_DIM, bytes_accessed=10 * query_in.size, transcendentals=pairs
        ),
    )(span_place, query_in, key_in, value_in, out_saved, out_grad)


def solution(mesh):
    placed = (
        P(("ctx", "head"), None),
        P("ctx", "head"),
        P("ctx", "head"),
        P(("ctx", "head"), None),
        P(("ctx", "head"), None),
        P(),
    )
    return jax.shard_map(
        body,
        mesh=mesh,
        in_specs=placed,
        out_specs=(P(("ctx", "head"), None), P("ctx", "head"), P("ctx", "head")),
        check_vma=False,
    )
```

```python
import functools
import math

import jax
import jax.numpy as jnp
from jax import lax
from jax.experimental import pallas as pl
from jax.experimental.pallas import tpu as pltpu
from jax.sharding import PartitionSpec as P

HEAD_DIM = 128
CORES = 2
GRANT = 56 * 1024 * 1024
MESH = pl.DeviceIdType.MESH
NT = (((1,), (1,)), ((), ()))
NN = (((1,), (0,)), ((), ()))
TN = (((0,), (0,)), ((), ()))


def matmul(a, b, dims):
    return lax.dot_general(a, b, dims, preferred_element_type=jnp.float32)


def columns(index):
    return pl.ds(pl.multiple_of(index * HEAD_DIM, HEAD_DIM), HEAD_DIM)


def kernel(
    ctx_size, head_size, place_in, query_in, key_in, value_in, saved_in, grad_in,
    dq_out, dk_out, dv_out,
    qbuf, gbuf, dbuf, kbuf, vbuf, pbuf, dk_stage, dv_stage, dq_stage, kpart, vpart, dk_total, dv_total,
    own_grad, own_saved, delta_src, place,
    send_sem, local_sem, q_sem, g_sem, d_sem, k_sem, v_sem, kp_sem, vp_sem, qp_sem,
):
    chips = ctx_size // CORES
    rows_high = max(chips // 2, 1)
    block = key_in.shape[0]
    token_rows = query_in.shape[0]
    heads = head_size * CORES
    rows = CORES * block
    span = ctx_size * block // place_in.shape[0]
    spans = rows // span
    scale = HEAD_DIM ** -0.5

    me = lax.axis_index("ctx")
    z = lax.axis_index("head")
    core = lax.rem(me, CORES)
    chip = me // CORES
    low, high = lax.rem(chip, 2), chip // 2

    def other_chip(step):
        return lax.rem(high + step // 2, rows_high) * 2 + lax.rem(low + step % 2, 2)

    def other_core(step):
        return lax.rem(core + step, CORES)

    def other_z(step):
        return lax.rem(z + step, head_size)

    chip_at = [other_chip(step) for step in range(chips)]
    core_at = [other_core(step) for step in range(CORES)]
    z_at = [other_z(step) for step in range(head_size)]
    plane = [(c, j) for c in range(chips) for j in range(CORES) if c or j]
    line = [(w, j) for w in range(head_size) for j in range(CORES) if w or j]

    def plane_id(c, j):
        return {"ctx": chip_at[c] * CORES + core_at[j], "head": z}

    def line_id(w, j):
        return {"ctx": chip * CORES + core_at[j], "head": z_at[w]}

    barrier = pltpu.get_barrier_semaphore()
    peers = [plane_id(c, j) for c, j in plane] + [line_id(w, j) for w, j in line if w]
    for peer in peers:
        pl.semaphore_signal(barrier, inc=1, device_id=peer, device_id_type=MESH)

    grad_load = pltpu.make_async_copy(grad_in, own_grad, local_sem.at[0])
    saved_load = pltpu.make_async_copy(saved_in, own_saved, local_sem.at[1])
    grad_load.start()
    saved_load.start()
    place_load = pltpu.make_async_copy(place_in, place, local_sem.at[2])
    place_load.start()
    my_head = z * CORES + core
    pltpu.make_async_copy(query_in.at[:, columns(my_head)], qbuf.at[core, z], q_sem.at[core, z]).start()
    pltpu.make_async_copy(key_in.at[:, columns(core)], kbuf.at[chip, core], k_sem.at[chip, core]).start()
    pltpu.make_async_copy(grad_in.at[:, columns(my_head)], gbuf.at[core, z], g_sem.at[core, z]).start()
    pltpu.make_async_copy(value_in.at[:, columns(core)], vbuf.at[chip, core], v_sem.at[chip, core]).start()

    grad_load.wait()
    saved_load.wait()
    product = own_grad[...].astype(jnp.float32) * own_saved[...].astype(jnp.float32)
    coarse = product.astype(jnp.bfloat16)
    fine = (product - coarse.astype(jnp.float32)).astype(jnp.bfloat16)
    shape = (heads, heads * HEAD_DIM)
    member = lax.broadcasted_iota(jnp.int32, shape, 1) // HEAD_DIM == lax.broadcasted_iota(jnp.int32, shape, 0)
    member = jnp.where(member, 1.0, 0.0).astype(jnp.bfloat16)
    delta = matmul(member, jnp.concatenate([coarse] * head_size, axis=0), NT)
    delta += matmul(member, jnp.concatenate([fine] * head_size, axis=0), NT)
    lane_z = lax.broadcasted_iota(jnp.int32, (heads, block), 1) // token_rows
    delta = jnp.where(lane_z == z, delta, 0.0)
    for h in range(heads):
        delta_src[h] = delta[h : h + 1]
    dbuf[core, z] = delta_src[my_head]

    pl.semaphore_wait(barrier, len(peers))

    sent = []

    def send(src, dst, sem, device):
        copy = pltpu.make_async_remote_copy(
            src_ref=src, dst_ref=dst, send_sem=send_sem.at[len(sent)], recv_sem=sem,
            device_id=device, device_id_type=MESH,
        )
        copy.start()
        sent.append(copy)

    def arrive(dst, sem):
        pltpu.make_async_copy(dst, dst, sem).wait()

    def send_plane(src, dst, sem):
        for c, j in plane[::-1]:
            send(src.at[:, columns(core_at[j])], dst.at[chip, core], sem.at[chip, core], plane_id(c, j))

    def send_line(src, dst, sem):
        for w, j in line:
            head = z_at[w] * CORES + core_at[j]
            send(src.at[:, columns(head)], dst.at[core, z], sem.at[core, z], line_id(w, j))

    send_line(query_in, qbuf, q_sem)
    send_plane(key_in, kbuf, k_sem)
    send_line(grad_in, gbuf, g_sem)
    send_plane(value_in, vbuf, v_sem)
    for w, j in line:
        head = z_at[w] * CORES + core_at[j]
        send(delta_src.at[head], dbuf.at[core, z], d_sem.at[core, z], line_id(w, j))

    place_load.wait()

    lane = lax.broadcasted_iota(jnp.int32, (1, rows), 1)
    place_row = jnp.zeros((1, rows), jnp.int32)
    for s in range(spans):
        place_row = jnp.where(lane // span == s, place[chip * spans + s], place_row)
    pos_row = place_row * span + lane % span
    within = lax.broadcasted_iota(jnp.int32, (span, rows), 0)

    for j in range(CORES):
        for w in range(head_size):
            arrive(qbuf.at[j, w], q_sem.at[j, w])
    query = qbuf[...].reshape(rows, HEAD_DIM)

    tops, sums = [], []
    for c in range(chips):
        for j in range(CORES):
            arrive(kbuf.at[chip_at[c], j], k_sem.at[chip_at[c], j])
        keys = kbuf[chip_at[c]].reshape(rows, HEAD_DIM)
        scores = matmul(keys, query, NT) * (scale * math.log2(math.e))
        pieces = []
        for s in range(spans):
            limit = pos_row - place[chip_at[c] * spans + s] * span
            pieces.append(jnp.where(within <= limit, scores[s * span : (s + 1) * span], -1e30))
        masked = jnp.concatenate(pieces, axis=0)
        top = jnp.max(masked, axis=0, keepdims=True)
        probs = jnp.exp2(masked - top)
        pbuf[c] = probs
        tops.append(top)
        sums.append(jnp.sum(probs, axis=0, keepdims=True))

    best = functools.reduce(jnp.maximum, tops)
    weights = [jnp.exp2(top - best) for top in tops]
    total = functools.reduce(jnp.add, [w * s for w, s in zip(weights, sums)])
    weights = [w / total for w in weights]

    for j in range(CORES):
        for w in range(head_size):
            arrive(gbuf.at[j, w], g_sem.at[j, w])
    grad = gbuf[...].reshape(rows, HEAD_DIM)
    for w, j in line:
        arrive(dbuf.at[core_at[j], z_at[w]], d_sem.at[core_at[j], z_at[w]])
    delta_row = jnp.concatenate(
        [functools.reduce(jnp.add, [dbuf[j, w] for w in range(head_size)]) for j in range(CORES)], axis=1
    )

    grad_q = jnp.zeros((rows, HEAD_DIM), jnp.float32)
    for c in range(chips)[::-1]:
        for j in range(CORES):
            arrive(vbuf.at[chip_at[c], j], v_sem.at[chip_at[c], j])
        values = vbuf[chip_at[c]].reshape(rows, HEAD_DIM)
        probs = pbuf[c] * weights[c]
        dv_stage[c] = matmul(probs.astype(jnp.bfloat16), grad, NN).astype(jnp.bfloat16).reshape(dv_stage.shape[1:])
        dprobs = matmul(values, grad, NT)
        dscores = (probs * (dprobs - delta_row) * scale).astype(jnp.bfloat16)
        dk_stage[c] = matmul(dscores, query, NN).astype(jnp.bfloat16).reshape(dk_stage.shape[1:])
        for stage, part, sem in ((dv_stage, vpart, vp_sem), (dk_stage, kpart, kp_sem)):
            for j in range(CORES):
                if c or j:
                    send(stage.at[c, core_at[j]], part.at[chip, core], sem.at[chip, core], plane_id(c, j))
                else:
                    part[chip, core] = stage[c, core]
        grad_q += matmul(dscores, kbuf[chip_at[c]].reshape(rows, HEAD_DIM), TN)

    dq_stage[...] = grad_q.astype(jnp.bfloat16).reshape(dq_stage.shape)
    for w, j in line:
        dst = dq_out.at[:, columns(my_head)]
        send(dq_stage.at[core_at[j], z_at[w]], dst, qp_sem.at[my_head], line_id(w, j))
    own = pltpu.make_async_copy(dq_stage.at[core, z], dq_out.at[:, columns(my_head)], qp_sem.at[my_head])
    own.start()

    stores = []
    for part, sem, total, out in ((vpart, vp_sem, dv_total, dv_out), (kpart, kp_sem, dk_total, dk_out)):
        for c, j in plane:
            arrive(part.at[chip_at[c], core_at[j]], sem.at[chip_at[c], core_at[j]])
        for j in range(CORES):
            summed = part[0, j].astype(jnp.float32)
            for c in range(1, chips):
                summed += part[c, j].astype(jnp.float32)
            total[:, j * HEAD_DIM : (j + 1) * HEAD_DIM] = summed.astype(jnp.bfloat16)
        stores.append(pltpu.make_async_copy(total, out, local_sem.at[len(stores)]))
        stores[-1].start()

    for h in range(heads):
        arrive(dq_out.at[:, h * HEAD_DIM : (h + 1) * HEAD_DIM], qp_sem.at[h])
    for copy in stores:
        copy.wait()
    for copy in sent:
        copy.wait_send()


def store_kernel(dq, dk, dv, dq_out, dk_out, dv_out, sem):
    pairs = ((dq, dq_out), (dk, dk_out), (dv, dv_out))
    copies = [pltpu.make_async_copy(src, dst, sem.at[i]) for i, (src, dst) in enumerate(pairs)]
    for copy in copies:
        copy.start()
    for copy in copies:
        copy.wait()


def body(query_in, key_in, value_in, out_saved, out_grad, span_place):
    ctx_size, head_size = lax.axis_size("ctx"), lax.axis_size("head")
    chips = ctx_size // CORES
    block = key_in.shape[0]
    token_rows, width = query_in.shape
    heads = head_size * CORES
    rows = CORES * block
    low = jnp.bfloat16
    tokens = (CORES, head_size, token_rows, HEAD_DIM)
    keys = (chips, CORES, block, HEAD_DIM)
    dma = pltpu.SemaphoreType.DMA
    copies = 4 * (ctx_size - 1) + 4 * (heads - 1)
    hbm = pl.BlockSpec(memory_space=pltpu.HBM)
    pairs = CORES * chips * rows * rows
    grads = pl.pallas_call(
        functools.partial(kernel, ctx_size, head_size),
        out_shape=(
            jax.ShapeDtypeStruct(query_in.shape, low),
            jax.ShapeDtypeStruct(key_in.shape, low),
            jax.ShapeDtypeStruct(value_in.shape, low),
        ),
        in_specs=[hbm] * 6,
        out_specs=(hbm, hbm, hbm),
        scratch_shapes=[
            pltpu.VMEM(tokens, low),
            pltpu.VMEM(tokens, low),
            pltpu.VMEM((CORES, head_size, 1, block), jnp.float32),
            pltpu.VMEM(keys, low),
            pltpu.VMEM(keys, low),
            pltpu.VMEM((chips, rows, rows), jnp.float32),
            pltpu.VMEM(keys, low),
            pltpu.VMEM(keys, low),
            pltpu.VMEM(tokens, low),
            pltpu.VMEM(keys, low),
            pltpu.VMEM(keys, low),
            pltpu.VMEM(key_in.shape, low),
            pltpu.VMEM(value_in.shape, low),
            pltpu.VMEM((token_rows, width), low),
            pltpu.VMEM((token_rows, width), low),
            pltpu.VMEM((heads, 1, block), jnp.float32),
            pltpu.SMEM(span_place.shape, span_place.dtype),
            dma((copies,)),
            dma((3,)),
            dma((CORES, head_size)),
            dma((CORES, head_size)),
            dma((CORES, head_size)),
            dma((chips, CORES)),
            dma((chips, CORES)),
            dma((chips, CORES)),
            dma((chips, CORES)),
            dma((heads,)),
        ],
        compiler_params=pltpu.CompilerParams(
            collective_id=0, has_side_effects=True, vmem_limit_bytes=GRANT
        ),
        cost_estimate=pl.CostEstimate(
            flops=5 * pairs * HEAD_DIM, bytes_accessed=10 * query_in.size, transcendentals=pairs
        ),
    )(span_place, query_in, key_in, value_in, out_saved, out_grad)
    return pl.pallas_call(
        store_kernel,
        out_shape=tuple(jax.ShapeDtypeStruct(g.shape, g.dtype) for g in grads),
        in_specs=[hbm] * 3,
        out_specs=(hbm, hbm, hbm),
        scratch_shapes=[dma((3,))],
        compiler_params=pltpu.CompilerParams(vmem_limit_bytes=GRANT),
    )(*grads)


def solution(mesh):
    placed = (
        P(("ctx", "head"), None),
        P("ctx", "head"),
        P("ctx", "head"),
        P(("ctx", "head"), None),
        P(("ctx", "head"), None),
        P(),
    )
    return jax.shard_map(
        body,
        mesh=mesh,
        in_specs=placed,
        out_specs=(P(("ctx", "head"), None), P("ctx", "head"), P("ctx", "head")),
        check_vma=False,
    )
```

```python
import functools
import math

import jax
import jax.numpy as jnp
from jax import lax
from jax.experimental import pallas as pl
from jax.experimental.pallas import tpu as pltpu
from jax.sharding import PartitionSpec as P

HEAD_DIM = 128
CORES = 2
GRANT = 56 * 1024 * 1024
MESH = pl.DeviceIdType.MESH
NT = (((1,), (1,)), ((), ()))
NN = (((1,), (0,)), ((), ()))
TN = (((0,), (0,)), ((), ()))


def matmul(a, b, dims):
    return lax.dot_general(a, b, dims, preferred_element_type=jnp.float32)


def columns(index):
    return pl.ds(pl.multiple_of(index * HEAD_DIM, HEAD_DIM), HEAD_DIM)


def kernel(
    ctx_size, head_size, place_in, query_in, key_in, value_in, saved_in, grad_in,
    dq_out, kpart, vpart,
    qbuf, gbuf, dbuf, kbuf, vbuf, pbuf, dk_stage, dv_stage, dq_stage,
    own_grad, own_saved, delta_src, place,
    send_sem, local_sem, q_sem, g_sem, d_sem, k_sem, v_sem, kp_sem, vp_sem, qp_sem,
):
    chips = ctx_size // CORES
    rows_high = max(chips // 2, 1)
    block = key_in.shape[0]
    token_rows = query_in.shape[0]
    heads = head_size * CORES
    rows = CORES * block
    span = ctx_size * block // place_in.shape[0]
    spans = rows // span
    scale = HEAD_DIM ** -0.5

    me = lax.axis_index("ctx")
    z = lax.axis_index("head")
    core = lax.rem(me, CORES)
    chip = me // CORES
    low, high = lax.rem(chip, 2), chip // 2

    def other_chip(step):
        return lax.rem(high + step // 2, rows_high) * 2 + lax.rem(low + step % 2, 2)

    def other_core(step):
        return lax.rem(core + step, CORES)

    def other_z(step):
        return lax.rem(z + step, head_size)

    chip_at = [other_chip(step) for step in range(chips)]
    core_at = [other_core(step) for step in range(CORES)]
    z_at = [other_z(step) for step in range(head_size)]
    plane = [(c, j) for c in range(chips) for j in range(CORES) if c or j]
    line = [(w, j) for w in range(head_size) for j in range(CORES) if w or j]

    def plane_id(c, j):
        return {"ctx": chip_at[c] * CORES + core_at[j], "head": z}

    def line_id(w, j):
        return {"ctx": chip * CORES + core_at[j], "head": z_at[w]}

    barrier = pltpu.get_barrier_semaphore()
    peers = [plane_id(c, j) for c, j in plane] + [line_id(w, j) for w, j in line if w]
    for peer in peers:
        pl.semaphore_signal(barrier, inc=1, device_id=peer, device_id_type=MESH)

    grad_load = pltpu.make_async_copy(grad_in, own_grad, local_sem.at[0])
    saved_load = pltpu.make_async_copy(saved_in, own_saved, local_sem.at[1])
    grad_load.start()
    saved_load.start()
    place_load = pltpu.make_async_copy(place_in, place, local_sem.at[2])
    place_load.start()
    my_head = z * CORES + core
    pltpu.make_async_copy(query_in.at[:, columns(my_head)], qbuf.at[core, z], q_sem.at[core, z]).start()
    pltpu.make_async_copy(key_in.at[:, columns(core)], kbuf.at[chip, core], k_sem.at[chip, core]).start()
    pltpu.make_async_copy(grad_in.at[:, columns(my_head)], gbuf.at[core, z], g_sem.at[core, z]).start()
    pltpu.make_async_copy(value_in.at[:, columns(core)], vbuf.at[chip, core], v_sem.at[chip, core]).start()

    grad_load.wait()
    saved_load.wait()
    product = own_grad[...].astype(jnp.float32) * own_saved[...].astype(jnp.float32)
    coarse = product.astype(jnp.bfloat16)
    fine = (product - coarse.astype(jnp.float32)).astype(jnp.bfloat16)
    shape = (heads, heads * HEAD_DIM)
    member = lax.broadcasted_iota(jnp.int32, shape, 1) // HEAD_DIM == lax.broadcasted_iota(jnp.int32, shape, 0)
    member = jnp.where(member, 1.0, 0.0).astype(jnp.bfloat16)
    delta = matmul(member, jnp.concatenate([coarse] * head_size, axis=0), NT)
    delta += matmul(member, jnp.concatenate([fine] * head_size, axis=0), NT)
    lane_z = lax.broadcasted_iota(jnp.int32, (heads, block), 1) // token_rows
    delta = jnp.where(lane_z == z, delta, 0.0)
    for h in range(heads):
        delta_src[h] = delta[h : h + 1]
    dbuf[core, z] = delta_src[my_head]

    pl.semaphore_wait(barrier, len(peers))

    sent = []

    def send(src, dst, sem, device):
        copy = pltpu.make_async_remote_copy(
            src_ref=src, dst_ref=dst, send_sem=send_sem.at[len(sent)], recv_sem=sem,
            device_id=device, device_id_type=MESH,
        )
        copy.start()
        sent.append(copy)

    def arrive(dst, sem):
        pltpu.make_async_copy(dst, dst, sem).wait()

    def send_plane(src, dst, sem):
        for c, j in plane[::-1]:
            send(src.at[:, columns(core_at[j])], dst.at[chip, core], sem.at[chip, core], plane_id(c, j))

    def send_line(src, dst, sem):
        for w, j in line:
            head = z_at[w] * CORES + core_at[j]
            send(src.at[:, columns(head)], dst.at[core, z], sem.at[core, z], line_id(w, j))

    send_line(query_in, qbuf, q_sem)
    send_plane(key_in, kbuf, k_sem)
    send_line(grad_in, gbuf, g_sem)
    send_plane(value_in, vbuf, v_sem)
    for w, j in line:
        head = z_at[w] * CORES + core_at[j]
        send(delta_src.at[head], dbuf.at[core, z], d_sem.at[core, z], line_id(w, j))

    place_load.wait()

    lane = lax.broadcasted_iota(jnp.int32, (1, rows), 1)
    place_row = jnp.zeros((1, rows), jnp.int32)
    for s in range(spans):
        place_row = jnp.where(lane // span == s, place[chip * spans + s], place_row)
    pos_row = place_row * span + lane % span
    within = lax.broadcasted_iota(jnp.int32, (span, rows), 0)

    for j in range(CORES):
        for w in range(head_size):
            arrive(qbuf.at[j, w], q_sem.at[j, w])
    query = qbuf[...].reshape(rows, HEAD_DIM)

    tops, sums = [], []
    for c in range(chips):
        for j in range(CORES):
            arrive(kbuf.at[chip_at[c], j], k_sem.at[chip_at[c], j])
        keys = kbuf[chip_at[c]].reshape(rows, HEAD_DIM)
        scores = matmul(keys, query, NT) * (scale * math.log2(math.e))
        pieces = []
        for s in range(spans):
            limit = pos_row - place[chip_at[c] * spans + s] * span
            pieces.append(jnp.where(within <= limit, scores[s * span : (s + 1) * span], -1e30))
        masked = jnp.concatenate(pieces, axis=0)
        top = jnp.max(masked, axis=0, keepdims=True)
        probs = jnp.exp2(masked - top)
        pbuf[c] = probs
        tops.append(top)
        sums.append(jnp.sum(probs, axis=0, keepdims=True))

    best = functools.reduce(jnp.maximum, tops)
    weights = [jnp.exp2(top - best) for top in tops]
    total = functools.reduce(jnp.add, [w * s for w, s in zip(weights, sums)])
    weights = [w / total for w in weights]

    for j in range(CORES):
        for w in range(head_size):
            arrive(gbuf.at[j, w], g_sem.at[j, w])
    grad = gbuf[...].reshape(rows, HEAD_DIM)
    for w, j in line:
        arrive(dbuf.at[core_at[j], z_at[w]], d_sem.at[core_at[j], z_at[w]])
    delta_row = jnp.concatenate(
        [functools.reduce(jnp.add, [dbuf[j, w] for w in range(head_size)]) for j in range(CORES)], axis=1
    )

    grad_q = jnp.zeros((rows, HEAD_DIM), jnp.float32)
    for c in range(chips)[::-1]:
        for j in range(CORES):
            arrive(vbuf.at[chip_at[c], j], v_sem.at[chip_at[c], j])
        values = vbuf[chip_at[c]].reshape(rows, HEAD_DIM)
        probs = pbuf[c] * weights[c]
        dv_stage[c] = matmul(probs.astype(jnp.bfloat16), grad, NN).astype(jnp.bfloat16).reshape(dv_stage.shape[1:])
        dprobs = matmul(values, grad, NT)
        dscores = (probs * (dprobs - delta_row) * scale).astype(jnp.bfloat16)
        dk_stage[c] = matmul(dscores, query, NN).astype(jnp.bfloat16).reshape(dk_stage.shape[1:])
        for stage, part, sem in ((dv_stage, vpart, vp_sem), (dk_stage, kpart, kp_sem)):
            for j in range(CORES):
                if c or j:
                    send(stage.at[c, core_at[j]], part.at[chip, core], sem.at[chip, core], plane_id(c, j))
                else:
                    pltpu.make_async_copy(stage.at[c, core], part.at[chip, core], sem.at[chip, core]).start()
        grad_q += matmul(dscores, kbuf[chip_at[c]].reshape(rows, HEAD_DIM), TN)

    dq_stage[...] = grad_q.astype(jnp.bfloat16).reshape(dq_stage.shape)
    for w, j in line:
        dst = dq_out.at[:, columns(my_head)]
        send(dq_stage.at[core_at[j], z_at[w]], dst, qp_sem.at[my_head], line_id(w, j))
    own = pltpu.make_async_copy(dq_stage.at[core, z], dq_out.at[:, columns(my_head)], qp_sem.at[my_head])
    own.start()

    for part, sem in ((vpart, vp_sem), (kpart, kp_sem)):
        for c in range(chips):
            for j in range(CORES):
                arrive(part.at[c, j], sem.at[c, j])
    for h in range(heads):
        arrive(dq_out.at[:, h * HEAD_DIM : (h + 1) * HEAD_DIM], qp_sem.at[h])
    for copy in sent:
        copy.wait_send()


def sum_kernel(dq, kpart, vpart, dq_out, dk_out, dv_out, dq_buf, kbuf, vbuf, dk_buf, dv_buf, load_sem, store_sem):
    loads = [
        pltpu.make_async_copy(src, dst, load_sem.at[i])
        for i, (src, dst) in enumerate(((vpart, vbuf), (kpart, kbuf), (dq, dq_buf)))
    ]
    for load in loads:
        load.start()
    stores = []
    for load, parts, total, out in ((loads[0], vbuf, dv_buf, dv_out), (loads[1], kbuf, dk_buf, dk_out)):
        load.wait()
        for j in range(parts.shape[1]):
            summed = parts[0, j].astype(jnp.float32)
            for c in range(1, parts.shape[0]):
                summed += parts[c, j].astype(jnp.float32)
            total[:, j * HEAD_DIM : (j + 1) * HEAD_DIM] = summed.astype(jnp.bfloat16)
        stores.append(pltpu.make_async_copy(total, out, store_sem.at[len(stores)]))
        stores[-1].start()
    loads[2].wait()
    stores.append(pltpu.make_async_copy(dq_buf, dq_out, store_sem.at[2]))
    stores[-1].start()
    for store in stores:
        store.wait()


def body(query_in, key_in, value_in, out_saved, out_grad, span_place):
    ctx_size, head_size = lax.axis_size("ctx"), lax.axis_size("head")
    chips = ctx_size // CORES
    block = key_in.shape[0]
    token_rows, width = query_in.shape
    heads = head_size * CORES
    rows = CORES * block
    low = jnp.bfloat16
    tokens = (CORES, head_size, token_rows, HEAD_DIM)
    keys = (chips, CORES, block, HEAD_DIM)
    dma = pltpu.SemaphoreType.DMA
    copies = 4 * (ctx_size - 1) + 4 * (heads - 1)
    hbm = pl.BlockSpec(memory_space=pltpu.HBM)
    pairs = CORES * chips * rows * rows
    grads = pl.pallas_call(
        functools.partial(kernel, ctx_size, head_size),
        out_shape=(
            jax.ShapeDtypeStruct(query_in.shape, low),
            jax.ShapeDtypeStruct(keys, low),
            jax.ShapeDtypeStruct(keys, low),
        ),
        in_specs=[hbm] * 6,
        out_specs=(hbm, hbm, hbm),
        scratch_shapes=[
            pltpu.VMEM(tokens, low),
            pltpu.VMEM(tokens, low),
            pltpu.VMEM((CORES, head_size, 1, block), jnp.float32),
            pltpu.VMEM(keys, low),
            pltpu.VMEM(keys, low),
            pltpu.VMEM((chips, rows, rows), jnp.float32),
            pltpu.VMEM(keys, low),
            pltpu.VMEM(keys, low),
            pltpu.VMEM(tokens, low),
            pltpu.VMEM((token_rows, width), low),
            pltpu.VMEM((token_rows, width), low),
            pltpu.VMEM((heads, 1, block), jnp.float32),
            pltpu.SMEM(span_place.shape, span_place.dtype),
            dma((copies,)),
            dma((3,)),
            dma((CORES, head_size)),
            dma((CORES, head_size)),
            dma((CORES, head_size)),
            dma((chips, CORES)),
            dma((chips, CORES)),
            dma((chips, CORES)),
            dma((chips, CORES)),
            dma((heads,)),
        ],
        compiler_params=pltpu.CompilerParams(
            collective_id=0, has_side_effects=True, vmem_limit_bytes=GRANT
        ),
        cost_estimate=pl.CostEstimate(
            flops=5 * pairs * HEAD_DIM, bytes_accessed=10 * query_in.size, transcendentals=pairs
        ),
    )(span_place, query_in, key_in, value_in, out_saved, out_grad)
    shapes = (query_in.shape, key_in.shape, value_in.shape)
    return pl.pallas_call(
        sum_kernel,
        out_shape=tuple(jax.ShapeDtypeStruct(shape, low) for shape in shapes),
        in_specs=[hbm] * 3,
        out_specs=(hbm, hbm, hbm),
        scratch_shapes=[
            pltpu.VMEM(query_in.shape, low),
            pltpu.VMEM(keys, low),
            pltpu.VMEM(keys, low),
            pltpu.VMEM(key_in.shape, low),
            pltpu.VMEM(value_in.shape, low),
            dma((3,)),
            dma((3,)),
        ],
        compiler_params=pltpu.CompilerParams(vmem_limit_bytes=GRANT),
    )(*grads)


def solution(mesh):
    placed = (
        P(("ctx", "head"), None),
        P("ctx", "head"),
        P("ctx", "head"),
        P(("ctx", "head"), None),
        P(("ctx", "head"), None),
        P(),
    )
    return jax.shard_map(
        body,
        mesh=mesh,
        in_specs=placed,
        out_specs=(P(("ctx", "head"), None), P("ctx", "head"), P("ctx", "head")),
        check_vma=False,
    )
```

```python
import functools
import math

import jax
import jax.numpy as jnp
from jax import lax
from jax.experimental import pallas as pl
from jax.experimental.pallas import tpu as pltpu
from jax.sharding import PartitionSpec as P

HEAD_DIM = 128
CORES = 2
SIDES = 2
GRANT = 56 * 1024 * 1024
MESH = pl.DeviceIdType.MESH
NT = (((1,), (1,)), ((), ()))
NN = (((1,), (0,)), ((), ()))
TN = (((0,), (0,)), ((), ()))


def matmul(a, b, dims):
    return lax.dot_general(a, b, dims, preferred_element_type=jnp.float32)


def columns(index):
    return pl.ds(pl.multiple_of(index * HEAD_DIM, HEAD_DIM), HEAD_DIM)


def kernel(
    ctx_size, head_size, place_in, query_in, key_in, value_in, saved_in, grad_in,
    qpart, kpart, vpart,
    qbuf, gbuf, dbuf, kbuf, vbuf, pbuf, dpbuf, plow, dslow, dk_stage, dv_stage, dq_stage,
    own_grad, own_saved, delta_src, stat_src, stat_got, place,
    send_sem, local_sem, q_sem, g_sem, d_sem, k_sem, v_sem, relay_sem, stat_sem, kp_sem, vp_sem, qp_sem,
):
    groups = kbuf.shape[0]
    block = key_in.shape[0]
    token_rows = query_in.shape[0]
    heads = head_size * CORES
    rows = CORES * block
    span = ctx_size * block // place_in.shape[0]
    spans = rows // span
    scale = HEAD_DIM ** -0.5

    me = lax.axis_index("ctx")
    z = lax.axis_index("head")
    core = lax.rem(me, CORES)
    chip = me // CORES
    low, high = lax.rem(chip, SIDES), chip // SIDES

    group_at = [lax.rem(high + step, groups) for step in range(groups)]
    side_at = [lax.rem(low + step, SIDES) for step in range(SIDES)]
    core_at = [lax.rem(core + step, CORES) for step in range(CORES)]
    z_at = [lax.rem(z + step, head_size) for step in range(head_size)]
    column = [(g, j) for g in range(groups) for j in range(CORES) if g or j]
    line = [(w, j) for w in range(head_size) for j in range(CORES) if w or j]
    every = [(w, j) for w in range(head_size) for j in range(CORES)]

    def column_id(g, j):
        return {"ctx": (group_at[g] * SIDES + low) * CORES + core_at[j], "head": z}

    def line_id(w, j, side=0):
        return {"ctx": (high * SIDES + side_at[side]) * CORES + core_at[j], "head": z_at[w]}

    barrier = pltpu.get_barrier_semaphore()
    peers = [column_id(g, j) for g, j in column] + [line_id(w, j) for w, j in line if w]
    peers += [line_id(w, j, 1) for w, j in every]
    for peer in peers:
        pl.semaphore_signal(barrier, inc=1, device_id=peer, device_id_type=MESH)

    grad_load = pltpu.make_async_copy(grad_in, own_grad, local_sem.at[0])
    saved_load = pltpu.make_async_copy(saved_in, own_saved, local_sem.at[1])
    grad_load.start()
    saved_load.start()
    place_load = pltpu.make_async_copy(place_in, place, local_sem.at[2])
    place_load.start()
    my_head = z * CORES + core
    pltpu.make_async_copy(query_in.at[:, columns(my_head)], qbuf.at[low, core, z], q_sem.at[core, z]).start()
    pltpu.make_async_copy(key_in.at[:, columns(core)], kbuf.at[high, core], k_sem.at[high, core]).start()
    pltpu.make_async_copy(grad_in.at[:, columns(my_head)], gbuf.at[low, core, z], g_sem.at[core, z]).start()
    pltpu.make_async_copy(value_in.at[:, columns(core)], vbuf.at[high, core], v_sem.at[high, core]).start()

    grad_load.wait()
    saved_load.wait()
    product = own_grad[...].astype(jnp.float32) * own_saved[...].astype(jnp.float32)
    coarse = product.astype(jnp.bfloat16)
    fine = (product - coarse.astype(jnp.float32)).astype(jnp.bfloat16)
    shape = (heads, heads * HEAD_DIM)
    member = lax.broadcasted_iota(jnp.int32, shape, 1) // HEAD_DIM == lax.broadcasted_iota(jnp.int32, shape, 0)
    member = jnp.where(member, 1.0, 0.0).astype(jnp.bfloat16)
    delta = matmul(member, jnp.concatenate([coarse] * head_size, axis=0), NT)
    delta += matmul(member, jnp.concatenate([fine] * head_size, axis=0), NT)
    lane_z = lax.broadcasted_iota(jnp.int32, (heads, block), 1) // token_rows
    delta = jnp.where(lane_z == z, delta, 0.0)
    for h in range(heads):
        delta_src[h] = delta[h : h + 1]
    dbuf[core, z] = delta_src[my_head]

    pl.semaphore_wait(barrier, len(peers))

    sent = []

    def send(src, dst, sem, device):
        copy = pltpu.make_async_remote_copy(
            src_ref=src, dst_ref=dst, send_sem=send_sem.at[len(sent)], recv_sem=sem,
            device_id=device, device_id_type=MESH,
        )
        copy.start()
        sent.append(copy)

    def arrive(dst, sem):
        pltpu.make_async_copy(dst, dst, sem).wait()

    def send_column(src, dst, sem):
        for g, j in column[::-1]:
            send(src.at[:, columns(core_at[j])], dst.at[high, core], sem.at[high, core], column_id(g, j))

    def send_line(src, dst, sem):
        for w, j in line:
            head = z_at[w] * CORES + core_at[j]
            send(src.at[:, columns(head)], dst.at[low, core, z], sem.at[core, z], line_id(w, j))

    def relay(buf, sem, first):
        for j in range(CORES):
            for w in range(head_size):
                arrive(buf.at[low, j, w], sem.at[j, w])
            send(buf.at[low, j], buf.at[low, j], relay_sem.at[first + j], line_id(0, 0, 1))

    def relayed(buf, first):
        for j in range(CORES):
            arrive(buf.at[side_at[1], j], relay_sem.at[first + j])

    def rows_of(buf, index):
        return buf[index].reshape(rows, HEAD_DIM)

    send_line(query_in, qbuf, q_sem)
    send_column(key_in, kbuf, k_sem)
    for w, j in line:
        head = z_at[w] * CORES + core_at[j]
        send(delta_src.at[head], dbuf.at[core, z], d_sem.at[core, z], line_id(w, j))
    send_line(grad_in, gbuf, g_sem)
    send_column(value_in, vbuf, v_sem)
    place_load.wait()

    lane = lax.broadcasted_iota(jnp.int32, (1, rows), 1)
    pos_row = []
    for side in range(SIDES):
        place_row = jnp.zeros((1, rows), jnp.int32)
        for s in range(spans):
            here = place[(high * SIDES + side_at[side]) * spans + s]
            place_row = jnp.where(lane // span == s, here, place_row)
        pos_row.append(place_row * span + lane % span)
    within = lax.broadcasted_iota(jnp.int32, (span, rows), 0)

    stats, tops = [], []
    for side in range(SIDES):
        if side == 0:
            relay(qbuf, q_sem, 0)
        else:
            relayed(qbuf, 0)
        query = rows_of(qbuf, side_at[side])
        side_tops, sums = [], []
        for g in range(groups):
            if side == 0:
                for j in range(CORES):
                    arrive(kbuf.at[group_at[g], j], k_sem.at[group_at[g], j])
            scores = matmul(rows_of(kbuf, group_at[g]), query, NT) * (scale * math.log2(math.e))
            pieces = []
            for s in range(spans):
                limit = pos_row[side] - place[(group_at[g] * SIDES + low) * spans + s] * span
                pieces.append(jnp.where(within <= limit, scores[s * span : (s + 1) * span], -1e30))
            masked = jnp.concatenate(pieces, axis=0)
            top = jnp.max(masked, axis=0, keepdims=True)
            probs = jnp.exp2(masked - top)
            pbuf[g, side] = probs
            side_tops.append(top)
            sums.append(jnp.sum(probs, axis=0, keepdims=True))
        best = functools.reduce(jnp.maximum, side_tops)
        total = functools.reduce(jnp.add, [jnp.exp2(t - best) * s for t, s in zip(side_tops, sums)])
        stats.append((best, total))
        tops.append(side_tops)

    for w, j in line:
        arrive(dbuf.at[core_at[j], z_at[w]], d_sem.at[core_at[j], z_at[w]])
    own_delta = jnp.concatenate(
        [functools.reduce(jnp.add, [dbuf[j, w] for w in range(head_size)]) for j in range(CORES)], axis=1
    )
    stat_src[...] = jnp.concatenate([*stats[0], *stats[1], own_delta, own_delta, own_delta, own_delta], axis=0)
    send(stat_src, stat_got, stat_sem.at[0], line_id(0, 0, 1))
    relay(gbuf, g_sem, CORES)

    for side in range(SIDES):
        if side:
            relayed(gbuf, CORES)
        grad = rows_of(gbuf, side_at[side])
        for g in range(groups):
            if side == 0:
                for j in range(CORES):
                    arrive(vbuf.at[group_at[g], j], v_sem.at[group_at[g], j])
            dpbuf[g, side] = matmul(rows_of(vbuf, group_at[g]), grad, NT)

    arrive(stat_got, stat_sem.at[0])
    got = stat_got[...]
    deltas = (own_delta, got[4:5])
    weights = []
    for side in range(SIDES):
        best, total = stats[side]
        their = 2 * (SIDES - 1 - side)
        their_best, their_total = got[their : their + 1], got[their + 1 : their + 2]
        top = jnp.maximum(best, their_best)
        total = total * jnp.exp2(best - top) + their_total * jnp.exp2(their_best - top)
        weights.append([jnp.exp2(t - top) / total for t in tops[side]])

    for side in range(SIDES)[::-1]:
        grad_q = jnp.zeros((rows, HEAD_DIM), jnp.float32)
        for g in range(groups):
            probs = pbuf[g, side] * weights[side][g]
            plow[g, side] = probs.astype(jnp.bfloat16)
            dscores = (probs * (dpbuf[g, side] - deltas[side]) * scale).astype(jnp.bfloat16)
            dslow[g, side] = dscores
            grad_q += matmul(dscores, rows_of(kbuf, group_at[g]), TN)
        dq_stage[side] = grad_q.astype(jnp.bfloat16).reshape(dq_stage.shape[1:])
        for w, j in every[::-1]:
            src, dst, sem = dq_stage.at[side, core_at[j], z_at[w]], qpart.at[low, my_head], qp_sem.at[low, my_head]
            if side or w or j:
                send(src, dst, sem, line_id(w, j, side))
            else:
                pltpu.make_async_copy(src, dst, sem).start()

    for g in range(groups)[::-1]:
        for low_part, stage, buf, part, sem in (
            (plow, dv_stage, gbuf, vpart, vp_sem),
            (dslow, dk_stage, qbuf, kpart, kp_sem),
        ):
            total = matmul(low_part[g, 0], rows_of(buf, side_at[0]), NN)
            total += matmul(low_part[g, 1], rows_of(buf, side_at[1]), NN)
            stage[g] = total.astype(jnp.bfloat16).reshape(stage.shape[1:])
            for j in range(CORES):
                src, dst = stage.at[g, core_at[j]], part.at[high, core]
                if g or j:
                    send(src, dst, sem.at[high, core], column_id(g, j))
                else:
                    pltpu.make_async_copy(src, dst, sem.at[high, core]).start()

    for part, sem in ((vpart, vp_sem), (kpart, kp_sem)):
        for g in range(groups):
            for j in range(CORES):
                arrive(part.at[g, j], sem.at[g, j])
    for side in range(SIDES):
        for h in range(heads):
            arrive(qpart.at[side, h], qp_sem.at[side, h])
    for copy in sent:
        copy.wait_send()


def sum_kernel(
    qpart, kpart, vpart, dq_out, dk_out, dv_out, qbuf, kbuf, vbuf, dq_buf, dk_buf, dv_buf, load_sem, store_sem
):
    loads = [
        pltpu.make_async_copy(src, dst, load_sem.at[i])
        for i, (src, dst) in enumerate(((vpart, vbuf), (kpart, kbuf), (qpart, qbuf)))
    ]
    for load in loads:
        load.start()
    stores = []
    for load, parts, total, out in ((loads[0], vbuf, dv_buf, dv_out), (loads[1], kbuf, dk_buf, dk_out)):
        load.wait()
        for j in range(parts.shape[1]):
            summed = parts[0, j].astype(jnp.float32)
            for c in range(1, parts.shape[0]):
                summed += parts[c, j].astype(jnp.float32)
            total[:, j * HEAD_DIM : (j + 1) * HEAD_DIM] = summed.astype(jnp.bfloat16)
        stores.append(pltpu.make_async_copy(total, out, store_sem.at[len(stores)]))
        stores[-1].start()
    loads[2].wait()
    for h in range(qbuf.shape[1]):
        summed = functools.reduce(jnp.add, [qbuf[side, h].astype(jnp.float32) for side in range(SIDES)])
        dq_buf[:, h * HEAD_DIM : (h + 1) * HEAD_DIM] = summed.astype(jnp.bfloat16)
    stores.append(pltpu.make_async_copy(dq_buf, dq_out, store_sem.at[2]))
    stores[-1].start()
    for store in stores:
        store.wait()


def body(query_in, key_in, value_in, out_saved, out_grad, span_place):
    ctx_size, head_size = lax.axis_size("ctx"), lax.axis_size("head")
    groups = ctx_size // (CORES * SIDES)
    block = key_in.shape[0]
    token_rows, width = query_in.shape
    heads = head_size * CORES
    rows = CORES * block
    low = jnp.bfloat16
    tokens = (SIDES, CORES, head_size, token_rows, HEAD_DIM)
    keys = (groups, CORES, block, HEAD_DIM)
    pieces = (SIDES, heads, token_rows, HEAD_DIM)
    tiles = (groups, SIDES, rows, rows)
    dma = pltpu.SemaphoreType.DMA
    copies = 4 * (CORES * groups - 1) + 3 * (heads - 1) + 2 * CORES + 1 + SIDES * heads - 1
    hbm = pl.BlockSpec(memory_space=pltpu.HBM)
    pairs = groups * SIDES * rows * rows
    grads = pl.pallas_call(
        functools.partial(kernel, ctx_size, head_size),
        out_shape=(
            jax.ShapeDtypeStruct(pieces, low),
            jax.ShapeDtypeStruct(keys, low),
            jax.ShapeDtypeStruct(keys, low),
        ),
        in_specs=[hbm] * 6,
        out_specs=(hbm, hbm, hbm),
        scratch_shapes=[
            pltpu.VMEM(tokens, low),
            pltpu.VMEM(tokens, low),
            pltpu.VMEM((CORES, head_size, 1, block), jnp.float32),
            pltpu.VMEM(keys, low),
            pltpu.VMEM(keys, low),
            pltpu.VMEM(tiles, jnp.float32),
            pltpu.VMEM(tiles, jnp.float32),
            pltpu.VMEM(tiles, low),
            pltpu.VMEM(tiles, low),
            pltpu.VMEM(keys, low),
            pltpu.VMEM(keys, low),
            pltpu.VMEM(tokens, low),
            pltpu.VMEM((token_rows, width), low),
            pltpu.VMEM((token_rows, width), low),
            pltpu.VMEM((heads, 1, block), jnp.float32),
            pltpu.VMEM((8, rows), jnp.float32),
            pltpu.VMEM((8, rows), jnp.float32),
            pltpu.SMEM(span_place.shape, span_place.dtype),
            dma((copies,)),
            dma((3,)),
            dma((CORES, head_size)),
            dma((CORES, head_size)),
            dma((CORES, head_size)),
            dma((groups, CORES)),
            dma((groups, CORES)),
            dma((2 * CORES,)),
            dma((1,)),
            dma((groups, CORES)),
            dma((groups, CORES)),
            dma((SIDES, heads)),
        ],
        compiler_params=pltpu.CompilerParams(
            collective_id=0, has_side_effects=True, vmem_limit_bytes=GRANT
        ),
        cost_estimate=pl.CostEstimate(
            flops=5 * pairs * HEAD_DIM, bytes_accessed=10 * query_in.size, transcendentals=pairs
        ),
    )(span_place, query_in, key_in, value_in, out_saved, out_grad)
    shapes = (query_in.shape, key_in.shape, value_in.shape)
    return pl.pallas_call(
        sum_kernel,
        out_shape=tuple(jax.ShapeDtypeStruct(shape, low) for shape in shapes),
        in_specs=[hbm] * 3,
        out_specs=(hbm, hbm, hbm),
        scratch_shapes=[
            pltpu.VMEM(pieces, low),
            pltpu.VMEM(keys, low),
            pltpu.VMEM(keys, low),
            pltpu.VMEM(query_in.shape, low),
            pltpu.VMEM(key_in.shape, low),
            pltpu.VMEM(value_in.shape, low),
            dma((3,)),
            dma((3,)),
        ],
        compiler_params=pltpu.CompilerParams(vmem_limit_bytes=GRANT),
    )(*grads)


def solution(mesh):
    placed = (
        P(("ctx", "head"), None),
        P("ctx", "head"),
        P("ctx", "head"),
        P(("ctx", "head"), None),
        P(("ctx", "head"), None),
        P(),
    )
    return jax.shard_map(
        body,
        mesh=mesh,
        in_specs=placed,
        out_specs=(P(("ctx", "head"), None), P("ctx", "head"), P("ctx", "head")),
        check_vma=False,
    )
```

```python
import functools
import math

import jax
import jax.numpy as jnp
from jax import lax
from jax.experimental import pallas as pl
from jax.experimental.pallas import tpu as pltpu
from jax.sharding import PartitionSpec as P

HEAD_DIM = 128
CORES = 2
DELTA_ROWS = 16
GRANT = 56 * 1024 * 1024
MESH = pl.DeviceIdType.MESH
NT = (((1,), (1,)), ((), ()))
NN = (((1,), (0,)), ((), ()))
TN = (((0,), (0,)), ((), ()))


def matmul(a, b, dims):
    return lax.dot_general(a, b, dims, preferred_element_type=jnp.float32)


def columns(index):
    return pl.ds(pl.multiple_of(index * HEAD_DIM, HEAD_DIM), HEAD_DIM)


def kernel(
    ctx_size, head_size, place_in, query_in, key_in, value_in, saved_in, grad_in,
    dq_out, parts,
    tbuf, kbuf, vbuf, pbuf, dp_stage, dq_stage,
    own_query, own_grad, own_saved, own_key, own_value, token_src, place,
    send_sem, local_sem, t_sem, k_sem, v_sem, p_sem, qp_sem,
):
    chips = ctx_size // CORES
    rows_high = max(chips // 2, 1)
    block = key_in.shape[0]
    token_rows = query_in.shape[0]
    heads = head_size * CORES
    rows = CORES * block
    span = ctx_size * block // place_in.shape[0]
    spans = rows // span
    scale = HEAD_DIM ** -0.5

    me = lax.axis_index("ctx")
    z = lax.axis_index("head")
    core = lax.rem(me, CORES)
    chip = me // CORES
    low, high = lax.rem(chip, 2), chip // 2

    def other_chip(step):
        return lax.rem(high + step // 2, rows_high) * 2 + lax.rem(low + step % 2, 2)

    def other_core(step):
        return lax.rem(core + step, CORES)

    def other_z(step):
        return lax.rem(z + step, head_size)

    chip_at = [other_chip(step) for step in range(chips)]
    core_at = [other_core(step) for step in range(CORES)]
    z_at = [other_z(step) for step in range(head_size)]
    plane = [(c, j) for c in range(chips) for j in range(CORES) if c or j]
    line = [(w, j) for w in range(head_size) for j in range(CORES) if w or j]

    def plane_id(c, j):
        return {"ctx": chip_at[c] * CORES + core_at[j], "head": z}

    def line_id(w, j):
        return {"ctx": chip * CORES + core_at[j], "head": z_at[w]}

    barrier = pltpu.get_barrier_semaphore()
    peers = [plane_id(c, j) for c, j in plane] + [line_id(w, j) for w, j in line if w]
    for peer in peers:
        pl.semaphore_signal(barrier, inc=1, device_id=peer, device_id_type=MESH)

    my_head = z * CORES + core
    held = (
        (grad_in, own_grad), (saved_in, own_saved), (query_in, own_query),
        (key_in, own_key), (value_in, own_value), (place_in, place),
    )
    loads = [pltpu.make_async_copy(src, dst, local_sem.at[i]) for i, (src, dst) in enumerate(held)]
    for load in loads:
        load.start()
    pltpu.make_async_copy(key_in.at[:, columns(core)], kbuf.at[chip, core], k_sem.at[chip, core]).start()
    pltpu.make_async_copy(value_in.at[:, columns(core)], vbuf.at[chip, core], v_sem.at[chip, core]).start()
    for load in loads:
        load.wait()

    product = own_grad[...].astype(jnp.float32) * own_saved[...].astype(jnp.float32)
    coarse = product.astype(jnp.bfloat16)
    fine = (product - coarse.astype(jnp.float32)).astype(jnp.bfloat16)
    shape = (heads, heads * HEAD_DIM)
    member = lax.broadcasted_iota(jnp.int32, shape, 1) // HEAD_DIM == lax.broadcasted_iota(jnp.int32, shape, 0)
    member = jnp.where(member, 1.0, 0.0).astype(jnp.bfloat16)
    delta = matmul(member, jnp.concatenate([coarse] * head_size, axis=0), NT)
    delta += matmul(member, jnp.concatenate([fine] * head_size, axis=0), NT)
    lane_z = lax.broadcasted_iota(jnp.int32, (heads, block), 1) // token_rows
    delta = jnp.where(lane_z == z, delta, 0.0)
    first = delta.astype(jnp.bfloat16).astype(jnp.float32)
    second = (delta - first).astype(jnp.bfloat16).astype(jnp.float32)
    third = delta - first - second
    padding = jnp.zeros((DELTA_ROWS - 3, block), jnp.float32)
    for h in range(heads):
        at = slice(h * HEAD_DIM, (h + 1) * HEAD_DIM)
        token_src[h, :token_rows] = own_query[:, at]
        token_src[h, token_rows : 2 * token_rows] = own_grad[:, at]
        split = jnp.concatenate([first[h : h + 1], second[h : h + 1], third[h : h + 1], padding], axis=0)
        token_src[h, 2 * token_rows :] = split.astype(jnp.bfloat16)
    tbuf[core, z] = token_src[my_head]

    pl.semaphore_wait(barrier, len(peers))

    sent = []

    def send(src, dst, sem, device):
        copy = pltpu.make_async_remote_copy(
            src_ref=src, dst_ref=dst, send_sem=send_sem.at[len(sent)], recv_sem=sem,
            device_id=device, device_id_type=MESH,
        )
        copy.start()
        sent.append(copy)

    def arrive(dst, sem):
        pltpu.make_async_copy(dst, dst, sem).wait()

    def send_plane(src, dst, sem):
        for c, j in plane:
            send(src.at[:, columns(core_at[j])], dst.at[chip, core], sem.at[chip, core], plane_id(c, j))

    for w, j in line:
        send(token_src.at[z_at[w] * CORES + core_at[j]], tbuf.at[core, z], t_sem.at[core, z], line_id(w, j))
    send_plane(own_key, kbuf, k_sem)
    send_plane(own_value, vbuf, v_sem)

    lane = lax.broadcasted_iota(jnp.int32, (1, rows), 1)
    place_row = jnp.zeros((1, rows), jnp.int32)
    for s in range(spans):
        place_row = jnp.where(lane // span == s, place[chip * spans + s], place_row)
    pos_row = place_row * span + lane % span
    within = lax.broadcasted_iota(jnp.int32, (span, rows), 0)

    for w, j in line:
        arrive(tbuf.at[core_at[j], z_at[w]], t_sem.at[core_at[j], z_at[w]])
    query = tbuf[:, :, :token_rows].reshape(rows, HEAD_DIM)
    grad = tbuf[:, :, token_rows : 2 * token_rows].reshape(rows, HEAD_DIM)
    delta_row = jnp.concatenate(
        [
            jnp.sum(
                functools.reduce(
                    jnp.add, [tbuf[j, w, 2 * token_rows :].astype(jnp.float32) for w in range(head_size)]
                ),
                axis=0, keepdims=True,
            )
            for j in range(CORES)
        ],
        axis=1,
    )

    tops, sums = [], []
    for c in range(chips):
        for j in range(CORES):
            arrive(kbuf.at[chip_at[c], j], k_sem.at[chip_at[c], j])
        keys = kbuf[chip_at[c]].reshape(rows, HEAD_DIM)
        scores = matmul(keys, query, NT) * (scale * math.log2(math.e))
        pieces = []
        for s in range(spans):
            limit = pos_row - place[chip_at[c] * spans + s] * span
            pieces.append(jnp.where(within <= limit, scores[s * span : (s + 1) * span], -1e30))
        masked = jnp.concatenate(pieces, axis=0)
        top = jnp.max(masked, axis=0, keepdims=True)
        probs = jnp.exp2(masked - top)
        pbuf[c] = probs
        tops.append(top)
        sums.append(jnp.sum(probs, axis=0, keepdims=True))

    best = functools.reduce(jnp.maximum, tops)
    weights = [jnp.exp2(top - best) for top in tops]
    total = functools.reduce(jnp.add, [w * s for w, s in zip(weights, sums)])
    weights = [w / total for w in weights]

    grad_q = jnp.zeros((rows, HEAD_DIM), jnp.float32)
    for c in range(chips):
        for j in range(CORES):
            arrive(vbuf.at[chip_at[c], j], v_sem.at[chip_at[c], j])
        values = vbuf[chip_at[c]].reshape(rows, HEAD_DIM)
        probs = pbuf[c] * weights[c]
        grad_v = matmul(probs.astype(jnp.bfloat16), grad, NN).astype(jnp.bfloat16)
        dprobs = matmul(values, grad, NT)
        dscores = (probs * (dprobs - delta_row) * scale).astype(jnp.bfloat16)
        grad_k = matmul(dscores, query, NN).astype(jnp.bfloat16)
        for j in range(CORES):
            dp_stage[c, j, 0] = grad_k[j * block : (j + 1) * block]
            dp_stage[c, j, 1] = grad_v[j * block : (j + 1) * block]
        for j in range(CORES):
            src, dst, sem = dp_stage.at[c, core_at[j]], parts.at[chip, core], p_sem.at[chip, core]
            if c or j:
                send(src, dst, sem, plane_id(c, j))
            else:
                pltpu.make_async_copy(src, dst, sem).start()
        grad_q += matmul(dscores, kbuf[chip_at[c]].reshape(rows, HEAD_DIM), TN)

    dq_stage[...] = grad_q.astype(jnp.bfloat16).reshape(dq_stage.shape)
    for w, j in line:
        dst = dq_out.at[:, columns(my_head)]
        send(dq_stage.at[core_at[j], z_at[w]], dst, qp_sem.at[my_head], line_id(w, j))
    own = pltpu.make_async_copy(dq_stage.at[core, z], dq_out.at[:, columns(my_head)], qp_sem.at[my_head])
    own.start()

    for c in range(chips):
        for j in range(CORES):
            arrive(parts.at[c, j], p_sem.at[c, j])
    for h in range(heads):
        arrive(dq_out.at[:, h * HEAD_DIM : (h + 1) * HEAD_DIM], qp_sem.at[h])
    for copy in sent:
        copy.wait_send()


def sum_kernel(dq, parts, dq_out, dk_out, dv_out, dq_buf, buf, dk_buf, dv_buf, load_sem, store_sem):
    chips, cores = parts.shape[:2]
    loads = [pltpu.make_async_copy(parts, buf, load_sem.at[0]), pltpu.make_async_copy(dq, dq_buf, load_sem.at[1])]
    for load in loads:
        load.start()
    loads[0].wait()
    stores = []
    for i, (total, out) in enumerate(((dk_buf, dk_out), (dv_buf, dv_out))):
        for j in range(cores):
            summed = buf[0, j, i].astype(jnp.float32)
            for c in range(1, chips):
                summed += buf[c, j, i].astype(jnp.float32)
            total[:, j * HEAD_DIM : (j + 1) * HEAD_DIM] = summed.astype(jnp.bfloat16)
        stores.append(pltpu.make_async_copy(total, out, store_sem.at[i]))
        stores[-1].start()
    loads[1].wait()
    stores.append(pltpu.make_async_copy(dq_buf, dq_out, store_sem.at[2]))
    stores[-1].start()
    for store in stores:
        store.wait()


def body(query_in, key_in, value_in, out_saved, out_grad, span_place):
    ctx_size, head_size = lax.axis_size("ctx"), lax.axis_size("head")
    chips = ctx_size // CORES
    block = key_in.shape[0]
    token_rows, width = query_in.shape
    heads = head_size * CORES
    rows = CORES * block
    low = jnp.bfloat16
    tokens = (CORES, head_size, token_rows, HEAD_DIM)
    message = (2 * token_rows + DELTA_ROWS, HEAD_DIM)
    keys = (chips, CORES, block, HEAD_DIM)
    pieces = (chips, CORES, 2, block, HEAD_DIM)
    dma = pltpu.SemaphoreType.DMA
    copies = 3 * (ctx_size - 1) + 2 * (heads - 1)
    hbm = pl.BlockSpec(memory_space=pltpu.HBM)
    pairs = CORES * chips * rows * rows
    grads = pl.pallas_call(
        functools.partial(kernel, ctx_size, head_size),
        out_shape=(jax.ShapeDtypeStruct(query_in.shape, low), jax.ShapeDtypeStruct(pieces, low)),
        in_specs=[hbm] * 6,
        out_specs=(hbm, hbm),
        scratch_shapes=[
            pltpu.VMEM((CORES, head_size, *message), low),
            pltpu.VMEM(keys, low),
            pltpu.VMEM(keys, low),
            pltpu.VMEM((chips, rows, rows), jnp.float32),
            pltpu.VMEM(pieces, low),
            pltpu.VMEM(tokens, low),
            pltpu.VMEM((token_rows, width), low),
            pltpu.VMEM((token_rows, width), low),
            pltpu.VMEM((token_rows, width), low),
            pltpu.VMEM(key_in.shape, low),
            pltpu.VMEM(value_in.shape, low),
            pltpu.VMEM((heads, *message), low),
            pltpu.SMEM(span_place.shape, span_place.dtype),
            dma((copies,)),
            dma((6,)),
            dma((CORES, head_size)),
            dma((chips, CORES)),
            dma((chips, CORES)),
            dma((chips, CORES)),
            dma((heads,)),
        ],
        compiler_params=pltpu.CompilerParams(
            collective_id=0, has_side_effects=True, vmem_limit_bytes=GRANT
        ),
        cost_estimate=pl.CostEstimate(
            flops=5 * pairs * HEAD_DIM, bytes_accessed=10 * query_in.size, transcendentals=pairs
        ),
    )(span_place, query_in, key_in, value_in, out_saved, out_grad)
    shapes = (query_in.shape, key_in.shape, value_in.shape)
    return pl.pallas_call(
        sum_kernel,
        out_shape=tuple(jax.ShapeDtypeStruct(shape, low) for shape in shapes),
        in_specs=[hbm] * 2,
        out_specs=(hbm, hbm, hbm),
        scratch_shapes=[
            pltpu.VMEM(query_in.shape, low),
            pltpu.VMEM(pieces, low),
            pltpu.VMEM(key_in.shape, low),
            pltpu.VMEM(value_in.shape, low),
            dma((2,)),
            dma((3,)),
        ],
        compiler_params=pltpu.CompilerParams(vmem_limit_bytes=GRANT),
    )(*grads)


def solution(mesh):
    placed = (
        P(("ctx", "head"), None),
        P("ctx", "head"),
        P("ctx", "head"),
        P(("ctx", "head"), None),
        P(("ctx", "head"), None),
        P(),
    )
    return jax.shard_map(
        body,
        mesh=mesh,
        in_specs=placed,
        out_specs=(P(("ctx", "head"), None), P("ctx", "head"), P("ctx", "head")),
        check_vma=False,
    )
```

```python
import functools
import math

import jax
import jax.numpy as jnp
from jax import lax
from jax.experimental import pallas as pl
from jax.experimental.pallas import tpu as pltpu
from jax.sharding import PartitionSpec as P

HEAD_DIM = 128
CORES = 2
DELTA_ROWS = 16
GRANT = 56 * 1024 * 1024
MESH = pl.DeviceIdType.MESH
NT = (((1,), (1,)), ((), ()))
NN = (((1,), (0,)), ((), ()))


def matmul(a, b, dims):
    return lax.dot_general(a, b, dims, preferred_element_type=jnp.float32)


def columns(index):
    return pl.ds(pl.multiple_of(index * HEAD_DIM, HEAD_DIM), HEAD_DIM)


def kernel(
    ctx_size, head_size, place_in, query_in, key_in, value_in, saved_in, grad_in,
    dq_out, parts,
    tbuf, kbuf, vbuf, key_cols, pbuf, plow, dslow, dp_stage, dq_stage,
    own_query, own_grad, own_saved, own_key, own_value, token_src, place,
    send_sem, local_sem, t_sem, k_sem, v_sem, p_sem, qp_sem,
):
    chips = ctx_size // CORES
    rows_high = max(chips // 2, 1)
    block = key_in.shape[0]
    token_rows = query_in.shape[0]
    heads = head_size * CORES
    rows = CORES * block
    span = ctx_size * block // place_in.shape[0]
    spans = rows // span
    scale = HEAD_DIM ** -0.5

    me = lax.axis_index("ctx")
    z = lax.axis_index("head")
    core = lax.rem(me, CORES)
    chip = me // CORES
    low, high = lax.rem(chip, 2), chip // 2

    def other_chip(step):
        return lax.rem(high + step // 2, rows_high) * 2 + lax.rem(low + step % 2, 2)

    def other_core(step):
        return lax.rem(core + step, CORES)

    def other_z(step):
        return lax.rem(z + step, head_size)

    chip_at = [other_chip(step) for step in range(chips)]
    core_at = [other_core(step) for step in range(CORES)]
    z_at = [other_z(step) for step in range(head_size)]
    plane = [(c, j) for c in range(chips) for j in range(CORES) if c or j]
    line = [(w, j) for w in range(head_size) for j in range(CORES) if w or j]

    def plane_id(c, j):
        return {"ctx": chip_at[c] * CORES + core_at[j], "head": z}

    def line_id(w, j):
        return {"ctx": chip * CORES + core_at[j], "head": z_at[w]}

    barrier = pltpu.get_barrier_semaphore()
    peers = [plane_id(c, j) for c, j in plane] + [line_id(w, j) for w, j in line if w]
    for peer in peers:
        pl.semaphore_signal(barrier, inc=1, device_id=peer, device_id_type=MESH)

    my_head = z * CORES + core
    held = (
        (grad_in, own_grad), (saved_in, own_saved), (query_in, own_query),
        (key_in, own_key), (value_in, own_value), (place_in, place),
    )
    loads = [pltpu.make_async_copy(src, dst, local_sem.at[i]) for i, (src, dst) in enumerate(held)]
    for load in loads:
        load.start()
    pltpu.make_async_copy(key_in.at[:, columns(core)], kbuf.at[chip, core], k_sem.at[chip, core]).start()
    pltpu.make_async_copy(value_in.at[:, columns(core)], vbuf.at[chip, core], v_sem.at[chip, core]).start()
    for load in loads:
        load.wait()

    product = own_grad[...].astype(jnp.float32) * own_saved[...].astype(jnp.float32)
    coarse = product.astype(jnp.bfloat16)
    fine = (product - coarse.astype(jnp.float32)).astype(jnp.bfloat16)
    shape = (heads, heads * HEAD_DIM)
    member = lax.broadcasted_iota(jnp.int32, shape, 1) // HEAD_DIM == lax.broadcasted_iota(jnp.int32, shape, 0)
    member = jnp.where(member, 1.0, 0.0).astype(jnp.bfloat16)
    delta = matmul(member, jnp.concatenate([coarse] * head_size, axis=0), NT)
    delta += matmul(member, jnp.concatenate([fine] * head_size, axis=0), NT)
    lane_z = lax.broadcasted_iota(jnp.int32, (heads, block), 1) // token_rows
    delta = jnp.where(lane_z == z, delta, 0.0)
    first = delta.astype(jnp.bfloat16).astype(jnp.float32)
    second = (delta - first).astype(jnp.bfloat16).astype(jnp.float32)
    third = delta - first - second
    padding = jnp.zeros((DELTA_ROWS - 3, block), jnp.float32)
    for h in range(heads):
        at = slice(h * HEAD_DIM, (h + 1) * HEAD_DIM)
        token_src[h, :token_rows] = own_query[:, at]
        token_src[h, token_rows : 2 * token_rows] = own_grad[:, at]
        split = jnp.concatenate([first[h : h + 1], second[h : h + 1], third[h : h + 1], padding], axis=0)
        token_src[h, 2 * token_rows :] = split.astype(jnp.bfloat16)
    tbuf[core, z] = token_src[my_head]

    pl.semaphore_wait(barrier, len(peers))

    sent = []

    def send(src, dst, sem, device):
        copy = pltpu.make_async_remote_copy(
            src_ref=src, dst_ref=dst, send_sem=send_sem.at[len(sent)], recv_sem=sem,
            device_id=device, device_id_type=MESH,
        )
        copy.start()
        sent.append(copy)

    def arrive(dst, sem):
        pltpu.make_async_copy(dst, dst, sem).wait()

    def send_plane(src, dst, sem):
        for c, j in plane:
            send(src.at[:, columns(core_at[j])], dst.at[chip, core], sem.at[chip, core], plane_id(c, j))

    for w, j in line:
        send(token_src.at[z_at[w] * CORES + core_at[j]], tbuf.at[core, z], t_sem.at[core, z], line_id(w, j))
    send_plane(own_key, kbuf, k_sem)
    send_plane(own_value, vbuf, v_sem)

    lane = lax.broadcasted_iota(jnp.int32, (1, rows), 1)
    place_row = jnp.zeros((1, rows), jnp.int32)
    for s in range(spans):
        place_row = jnp.where(lane // span == s, place[chip * spans + s], place_row)
    pos_row = place_row * span + lane % span
    within = lax.broadcasted_iota(jnp.int32, (span, rows), 0)

    for w, j in line:
        arrive(tbuf.at[core_at[j], z_at[w]], t_sem.at[core_at[j], z_at[w]])
    query = tbuf[:, :, :token_rows].reshape(rows, HEAD_DIM)
    grad = tbuf[:, :, token_rows : 2 * token_rows].reshape(rows, HEAD_DIM)
    delta_row = jnp.concatenate(
        [
            jnp.sum(
                functools.reduce(
                    jnp.add, [tbuf[j, w, 2 * token_rows :].astype(jnp.float32) for w in range(head_size)]
                ),
                axis=0, keepdims=True,
            )
            for j in range(CORES)
        ],
        axis=1,
    )

    query_cols = query.T
    grad_cols = grad.T

    def chunk(buf, c):
        return buf[chip_at[c]].reshape(rows, HEAD_DIM)

    for c in range(chips):
        for j in range(CORES):
            arrive(kbuf.at[chip_at[c], j], k_sem.at[chip_at[c], j])
    tops, sums = [], []
    for c in range(chips):
        keys = chunk(kbuf, c)
        key_cols[:, c * rows : (c + 1) * rows] = keys.T
        scores = matmul(keys, query_cols, NN) * (scale * math.log2(math.e))
        pieces = []
        for s in range(spans):
            limit = pos_row - place[chip_at[c] * spans + s] * span
            pieces.append(jnp.where(within <= limit, scores[s * span : (s + 1) * span], -1e30))
        masked = jnp.concatenate(pieces, axis=0)
        top = jnp.max(masked, axis=0, keepdims=True)
        probs = jnp.exp2(masked - top)
        pbuf[c] = probs
        tops.append(top)
        sums.append(jnp.sum(probs, axis=0, keepdims=True))

    best = functools.reduce(jnp.maximum, tops)
    weights = [jnp.exp2(top - best) for top in tops]
    total = functools.reduce(jnp.add, [w * s for w, s in zip(weights, sums)])
    weights = [w / total for w in weights]

    for c in range(chips):
        for j in range(CORES):
            arrive(vbuf.at[chip_at[c], j], v_sem.at[chip_at[c], j])

    def score_grads(c):
        probs = pbuf[c] * weights[c]
        plow[c] = probs.astype(jnp.bfloat16)
        dprobs = matmul(chunk(vbuf, c), grad_cols, NN)
        dslow[c * rows : (c + 1) * rows] = (probs * (dprobs - delta_row) * scale).astype(jnp.bfloat16)

    def key_grads(c):
        grad_v = matmul(plow[c], grad, NN).astype(jnp.bfloat16)
        grad_k = matmul(dslow[c * rows : (c + 1) * rows], query, NN).astype(jnp.bfloat16)
        for j in range(CORES):
            dp_stage[c, j, 0] = grad_k[j * block : (j + 1) * block]
            dp_stage[c, j, 1] = grad_v[j * block : (j + 1) * block]

    def send_key_grads(c):
        for j in range(CORES):
            src, dst, sem = dp_stage.at[c, core_at[j]], parts.at[chip, core], p_sem.at[chip, core]
            if c or j:
                send(src, dst, sem, plane_id(c, j))
            else:
                pltpu.make_async_copy(src, dst, sem).start()

    order = list(range(chips))[::-1]
    score_grads(order[0])
    for now, later in zip(order, order[1:]):
        key_grads(now)
        score_grads(later)
        send_key_grads(now)

    grad_q = matmul(key_cols[...], dslow[...], NN).T
    dq_stage[...] = grad_q.astype(jnp.bfloat16).reshape(dq_stage.shape)
    for w, j in line:
        dst = dq_out.at[:, columns(my_head)]
        send(dq_stage.at[core_at[j], z_at[w]], dst, qp_sem.at[my_head], line_id(w, j))
    own = pltpu.make_async_copy(dq_stage.at[core, z], dq_out.at[:, columns(my_head)], qp_sem.at[my_head])
    own.start()
    key_grads(0)
    send_key_grads(0)

    for c in range(chips):
        for j in range(CORES):
            arrive(parts.at[c, j], p_sem.at[c, j])
    for h in range(heads):
        arrive(dq_out.at[:, h * HEAD_DIM : (h + 1) * HEAD_DIM], qp_sem.at[h])
    for copy in sent:
        copy.wait_send()


def sum_kernel(dq, parts, dq_out, dk_out, dv_out, dq_buf, buf, dk_buf, dv_buf, load_sem, store_sem):
    chips, cores = parts.shape[:2]
    loads = [pltpu.make_async_copy(parts, buf, load_sem.at[0]), pltpu.make_async_copy(dq, dq_buf, load_sem.at[1])]
    for load in loads:
        load.start()
    loads[0].wait()
    stores = []
    for i, (total, out) in enumerate(((dk_buf, dk_out), (dv_buf, dv_out))):
        for j in range(cores):
            summed = buf[0, j, i].astype(jnp.float32)
            for c in range(1, chips):
                summed += buf[c, j, i].astype(jnp.float32)
            total[:, j * HEAD_DIM : (j + 1) * HEAD_DIM] = summed.astype(jnp.bfloat16)
        stores.append(pltpu.make_async_copy(total, out, store_sem.at[i]))
        stores[-1].start()
    loads[1].wait()
    stores.append(pltpu.make_async_copy(dq_buf, dq_out, store_sem.at[2]))
    stores[-1].start()
    for store in stores:
        store.wait()


def body(query_in, key_in, value_in, out_saved, out_grad, span_place):
    ctx_size, head_size = lax.axis_size("ctx"), lax.axis_size("head")
    chips = ctx_size // CORES
    block = key_in.shape[0]
    token_rows, width = query_in.shape
    heads = head_size * CORES
    rows = CORES * block
    low = jnp.bfloat16
    tokens = (CORES, head_size, token_rows, HEAD_DIM)
    message = (2 * token_rows + DELTA_ROWS, HEAD_DIM)
    keys = (chips, CORES, block, HEAD_DIM)
    pieces = (chips, CORES, 2, block, HEAD_DIM)
    dma = pltpu.SemaphoreType.DMA
    copies = 3 * (ctx_size - 1) + 2 * (heads - 1)
    hbm = pl.BlockSpec(memory_space=pltpu.HBM)
    pairs = CORES * chips * rows * rows
    grads = pl.pallas_call(
        functools.partial(kernel, ctx_size, head_size),
        out_shape=(jax.ShapeDtypeStruct(query_in.shape, low), jax.ShapeDtypeStruct(pieces, low)),
        in_specs=[hbm] * 6,
        out_specs=(hbm, hbm),
        scratch_shapes=[
            pltpu.VMEM((CORES, head_size, *message), low),
            pltpu.VMEM(keys, low),
            pltpu.VMEM(keys, low),
            pltpu.VMEM((HEAD_DIM, chips * rows), low),
            pltpu.VMEM((chips, rows, rows), jnp.float32),
            pltpu.VMEM((chips, rows, rows), low),
            pltpu.VMEM((chips * rows, rows), low),
            pltpu.VMEM(pieces, low),
            pltpu.VMEM(tokens, low),
            pltpu.VMEM((token_rows, width), low),
            pltpu.VMEM((token_rows, width), low),
            pltpu.VMEM((token_rows, width), low),
            pltpu.VMEM(key_in.shape, low),
            pltpu.VMEM(value_in.shape, low),
            pltpu.VMEM((heads, *message), low),
            pltpu.SMEM(span_place.shape, span_place.dtype),
            dma((copies,)),
            dma((6,)),
            dma((CORES, head_size)),
            dma((chips, CORES)),
            dma((chips, CORES)),
            dma((chips, CORES)),
            dma((heads,)),
        ],
        compiler_params=pltpu.CompilerParams(
            collective_id=0, has_side_effects=True, vmem_limit_bytes=GRANT
        ),
        cost_estimate=pl.CostEstimate(
            flops=5 * pairs * HEAD_DIM, bytes_accessed=10 * query_in.size, transcendentals=pairs
        ),
    )(span_place, query_in, key_in, value_in, out_saved, out_grad)
    shapes = (query_in.shape, key_in.shape, value_in.shape)
    return pl.pallas_call(
        sum_kernel,
        out_shape=tuple(jax.ShapeDtypeStruct(shape, low) for shape in shapes),
        in_specs=[hbm] * 2,
        out_specs=(hbm, hbm, hbm),
        scratch_shapes=[
            pltpu.VMEM(query_in.shape, low),
            pltpu.VMEM(pieces, low),
            pltpu.VMEM(key_in.shape, low),
            pltpu.VMEM(value_in.shape, low),
            dma((2,)),
            dma((3,)),
        ],
        compiler_params=pltpu.CompilerParams(vmem_limit_bytes=GRANT),
    )(*grads)


def solution(mesh):
    placed = (
        P(("ctx", "head"), None),
        P("ctx", "head"),
        P("ctx", "head"),
        P(("ctx", "head"), None),
        P(("ctx", "head"), None),
        P(),
    )
    return jax.shard_map(
        body,
        mesh=mesh,
        in_specs=placed,
        out_specs=(P(("ctx", "head"), None), P("ctx", "head"), P("ctx", "head")),
        check_vma=False,
    )
```

```python
import functools
import math

import jax
import jax.numpy as jnp
from jax import lax
from jax.experimental import pallas as pl
from jax.experimental.pallas import tpu as pltpu
from jax.sharding import PartitionSpec as P

HEAD_DIM = 128
CORES = 2
DELTA_ROWS = 16
GRANT = 56 * 1024 * 1024
MESH = pl.DeviceIdType.MESH
NT = (((1,), (1,)), ((), ()))
NN = (((1,), (0,)), ((), ()))


def matmul(a, b, dims):
    return lax.dot_general(a, b, dims, preferred_element_type=jnp.float32)


def columns(index):
    return pl.ds(pl.multiple_of(index * HEAD_DIM, HEAD_DIM), HEAD_DIM)


def kernel(
    ctx_size, head_size, place_in, query_in, key_in, value_in, saved_in, grad_in,
    dq_out, parts,
    tbuf, kbuf, vbuf, key_cols, pbuf, dp_stage, dq_stage,
    own_query, own_grad, own_saved, own_key, own_value, token_src, place,
    send_sem, local_sem, t_sem, k_sem, v_sem, p_sem, qp_sem,
):
    chips = ctx_size // CORES
    rows_high = max(chips // 2, 1)
    block = key_in.shape[0]
    token_rows = query_in.shape[0]
    heads = head_size * CORES
    rows = CORES * block
    span = ctx_size * block // place_in.shape[0]
    spans = rows // span
    scale = HEAD_DIM ** -0.5

    me = lax.axis_index("ctx")
    z = lax.axis_index("head")
    core = lax.rem(me, CORES)
    chip = me // CORES
    low, high = lax.rem(chip, 2), chip // 2

    def other_chip(step):
        return lax.rem(high + step // 2, rows_high) * 2 + lax.rem(low + step % 2, 2)

    def other_core(step):
        return lax.rem(core + step, CORES)

    def other_z(step):
        return lax.rem(z + step, head_size)

    chip_at = [other_chip(step) for step in range(chips)]
    core_at = [other_core(step) for step in range(CORES)]
    z_at = [other_z(step) for step in range(head_size)]
    plane = [(c, j) for c in range(chips) for j in range(CORES) if c or j]
    line = [(w, j) for w in range(head_size) for j in range(CORES) if w or j]

    def plane_id(c, j):
        return {"ctx": chip_at[c] * CORES + core_at[j], "head": z}

    def line_id(w, j):
        return {"ctx": chip * CORES + core_at[j], "head": z_at[w]}

    barrier = pltpu.get_barrier_semaphore()
    peers = [plane_id(c, j) for c, j in plane] + [line_id(w, j) for w, j in line if w]
    for peer in peers:
        pl.semaphore_signal(barrier, inc=1, device_id=peer, device_id_type=MESH)

    my_head = z * CORES + core
    held = (
        (grad_in, own_grad), (saved_in, own_saved), (query_in, own_query),
        (key_in, own_key), (value_in, own_value), (place_in, place),
    )
    loads = [pltpu.make_async_copy(src, dst, local_sem.at[i]) for i, (src, dst) in enumerate(held)]
    for load in loads:
        load.start()
    pltpu.make_async_copy(key_in.at[:, columns(core)], kbuf.at[chip, core], k_sem.at[chip, core]).start()
    pltpu.make_async_copy(value_in.at[:, columns(core)], vbuf.at[chip, core], v_sem.at[chip, core]).start()
    for load in loads:
        load.wait()

    product = own_grad[...].astype(jnp.float32) * own_saved[...].astype(jnp.float32)
    coarse = product.astype(jnp.bfloat16)
    fine = (product - coarse.astype(jnp.float32)).astype(jnp.bfloat16)
    shape = (heads, heads * HEAD_DIM)
    member = lax.broadcasted_iota(jnp.int32, shape, 1) // HEAD_DIM == lax.broadcasted_iota(jnp.int32, shape, 0)
    member = jnp.where(member, 1.0, 0.0).astype(jnp.bfloat16)
    delta = matmul(member, jnp.concatenate([coarse] * head_size, axis=0), NT)
    delta += matmul(member, jnp.concatenate([fine] * head_size, axis=0), NT)
    lane_z = lax.broadcasted_iota(jnp.int32, (heads, block), 1) // token_rows
    delta = jnp.where(lane_z == z, delta, 0.0)
    first = delta.astype(jnp.bfloat16).astype(jnp.float32)
    second = (delta - first).astype(jnp.bfloat16).astype(jnp.float32)
    third = delta - first - second
    padding = jnp.zeros((DELTA_ROWS - 3, block), jnp.float32)
    for h in range(heads):
        at = slice(h * HEAD_DIM, (h + 1) * HEAD_DIM)
        token_src[h, :token_rows] = own_query[:, at]
        token_src[h, token_rows : 2 * token_rows] = own_grad[:, at]
        split = jnp.concatenate([first[h : h + 1], second[h : h + 1], third[h : h + 1], padding], axis=0)
        token_src[h, 2 * token_rows :] = split.astype(jnp.bfloat16)
    tbuf[core, z] = token_src[my_head]

    pl.semaphore_wait(barrier, len(peers))

    sent = []

    def send(src, dst, sem, device):
        copy = pltpu.make_async_remote_copy(
            src_ref=src, dst_ref=dst, send_sem=send_sem.at[len(sent)], recv_sem=sem,
            device_id=device, device_id_type=MESH,
        )
        copy.start()
        sent.append(copy)

    def arrive(dst, sem):
        pltpu.make_async_copy(dst, dst, sem).wait()

    def send_plane(src, dst, sem):
        for c, j in plane[::-1]:
            send(src.at[:, columns(core_at[j])], dst.at[chip, core], sem.at[chip, core], plane_id(c, j))

    for w, j in line:
        send(token_src.at[z_at[w] * CORES + core_at[j]], tbuf.at[core, z], t_sem.at[core, z], line_id(w, j))
    send_plane(own_key, kbuf, k_sem)
    send_plane(own_value, vbuf, v_sem)

    lane = lax.broadcasted_iota(jnp.int32, (1, rows), 1)
    place_row = jnp.zeros((1, rows), jnp.int32)
    for s in range(spans):
        place_row = jnp.where(lane // span == s, place[chip * spans + s], place_row)
    pos_row = place_row * span + lane % span
    within = lax.broadcasted_iota(jnp.int32, (span, rows), 0)

    for w, j in line:
        arrive(tbuf.at[core_at[j], z_at[w]], t_sem.at[core_at[j], z_at[w]])
    query = tbuf[:, :, :token_rows].reshape(rows, HEAD_DIM)
    grad = tbuf[:, :, token_rows : 2 * token_rows].reshape(rows, HEAD_DIM)
    delta_row = jnp.concatenate(
        [
            jnp.sum(
                functools.reduce(
                    jnp.add, [tbuf[j, w, 2 * token_rows :].astype(jnp.float32) for w in range(head_size)]
                ),
                axis=0, keepdims=True,
            )
            for j in range(CORES)
        ],
        axis=1,
    )

    query_cols = query.T
    grad_cols = grad.T

    def chunk(buf, c):
        return buf[chip_at[c]].reshape(rows, HEAD_DIM)

    tops, sums = [], []
    for c in range(chips):
        for j in range(CORES):
            arrive(kbuf.at[chip_at[c], j], k_sem.at[chip_at[c], j])
        keys = chunk(kbuf, c)
        key_cols[:, c * rows : (c + 1) * rows] = keys.T
        scores = matmul(keys, query_cols, NN) * (scale * math.log2(math.e))
        pieces = []
        for s in range(spans):
            limit = pos_row - place[chip_at[c] * spans + s] * span
            pieces.append(jnp.where(within <= limit, scores[s * span : (s + 1) * span], -1e30))
        masked = jnp.concatenate(pieces, axis=0)
        top = jnp.max(masked, axis=0, keepdims=True)
        probs = jnp.exp2(masked - top)
        pbuf[c] = probs
        tops.append(top)
        sums.append(jnp.sum(probs, axis=0, keepdims=True))

    best = functools.reduce(jnp.maximum, tops)
    weights = [jnp.exp2(top - best) for top in tops]
    total = functools.reduce(jnp.add, [w * s for w, s in zip(weights, sums)])
    weights = [w / total for w in weights]

    def send_part(c, kind, total):
        total = total.astype(jnp.bfloat16)
        for j in range(CORES):
            dp_stage[c, j, kind] = total[j * block : (j + 1) * block]
        for j in range(CORES):
            src, dst = dp_stage.at[c, core_at[j], kind], parts.at[chip, core, kind]
            if c or j:
                send(src, dst, p_sem.at[kind, chip, core], plane_id(c, j))
            else:
                pltpu.make_async_copy(src, dst, p_sem.at[kind, chip, core]).start()

    far_first = list(range(chips))[::-1]
    for c in far_first:
        probs = pbuf[c] * weights[c]
        pbuf[c] = probs
        send_part(c, 1, matmul(probs.astype(jnp.bfloat16), grad, NN))

    grad_q = jnp.zeros((HEAD_DIM, rows), jnp.float32)
    for c in far_first[-1:] + far_first[:-1]:
        for j in range(CORES):
            arrive(vbuf.at[chip_at[c], j], v_sem.at[chip_at[c], j])
        dprobs = matmul(chunk(vbuf, c), grad_cols, NN)
        dscores = (pbuf[c] * (dprobs - delta_row) * scale).astype(jnp.bfloat16)
        send_part(c, 0, matmul(dscores, query, NN))
        grad_q += matmul(key_cols[:, c * rows : (c + 1) * rows], dscores, NN)
    grad_q = grad_q.T

    dq_stage[...] = grad_q.astype(jnp.bfloat16).reshape(dq_stage.shape)
    for w, j in line:
        dst = dq_out.at[:, columns(my_head)]
        send(dq_stage.at[core_at[j], z_at[w]], dst, qp_sem.at[my_head], line_id(w, j))
    own = pltpu.make_async_copy(dq_stage.at[core, z], dq_out.at[:, columns(my_head)], qp_sem.at[my_head])
    own.start()

    for c in range(chips):
        for j in range(CORES):
            for kind in range(2):
                arrive(parts.at[c, j, kind], p_sem.at[kind, c, j])
    for h in range(heads):
        arrive(dq_out.at[:, h * HEAD_DIM : (h + 1) * HEAD_DIM], qp_sem.at[h])
    for copy in sent:
        copy.wait_send()


def sum_kernel(dq, parts, dq_out, dk_out, dv_out, dq_buf, buf, dk_buf, dv_buf, load_sem, store_sem):
    chips, cores = parts.shape[:2]
    loads = [pltpu.make_async_copy(parts, buf, load_sem.at[0]), pltpu.make_async_copy(dq, dq_buf, load_sem.at[1])]
    for load in loads:
        load.start()
    loads[0].wait()
    stores = []
    for i, (total, out) in enumerate(((dk_buf, dk_out), (dv_buf, dv_out))):
        for j in range(cores):
            summed = buf[0, j, i].astype(jnp.float32)
            for c in range(1, chips):
                summed += buf[c, j, i].astype(jnp.float32)
            total[:, j * HEAD_DIM : (j + 1) * HEAD_DIM] = summed.astype(jnp.bfloat16)
        stores.append(pltpu.make_async_copy(total, out, store_sem.at[i]))
        stores[-1].start()
    loads[1].wait()
    stores.append(pltpu.make_async_copy(dq_buf, dq_out, store_sem.at[2]))
    stores[-1].start()
    for store in stores:
        store.wait()


def body(query_in, key_in, value_in, out_saved, out_grad, span_place):
    ctx_size, head_size = lax.axis_size("ctx"), lax.axis_size("head")
    chips = ctx_size // CORES
    block = key_in.shape[0]
    token_rows, width = query_in.shape
    heads = head_size * CORES
    rows = CORES * block
    low = jnp.bfloat16
    tokens = (CORES, head_size, token_rows, HEAD_DIM)
    message = (2 * token_rows + DELTA_ROWS, HEAD_DIM)
    keys = (chips, CORES, block, HEAD_DIM)
    pieces = (chips, CORES, 2, block, HEAD_DIM)
    dma = pltpu.SemaphoreType.DMA
    copies = 4 * (ctx_size - 1) + 2 * (heads - 1)
    hbm = pl.BlockSpec(memory_space=pltpu.HBM)
    pairs = CORES * chips * rows * rows
    grads = pl.pallas_call(
        functools.partial(kernel, ctx_size, head_size),
        out_shape=(jax.ShapeDtypeStruct(query_in.shape, low), jax.ShapeDtypeStruct(pieces, low)),
        in_specs=[hbm] * 6,
        out_specs=(hbm, hbm),
        scratch_shapes=[
            pltpu.VMEM((CORES, head_size, *message), low),
            pltpu.VMEM(keys, low),
            pltpu.VMEM(keys, low),
            pltpu.VMEM((HEAD_DIM, chips * rows), low),
            pltpu.VMEM((chips, rows, rows), jnp.float32),
            pltpu.VMEM(pieces, low),
            pltpu.VMEM(tokens, low),
            pltpu.VMEM((token_rows, width), low),
            pltpu.VMEM((token_rows, width), low),
            pltpu.VMEM((token_rows, width), low),
            pltpu.VMEM(key_in.shape, low),
            pltpu.VMEM(value_in.shape, low),
            pltpu.VMEM((heads, *message), low),
            pltpu.SMEM(span_place.shape, span_place.dtype),
            dma((copies,)),
            dma((6,)),
            dma((CORES, head_size)),
            dma((chips, CORES)),
            dma((chips, CORES)),
            dma((2, chips, CORES)),
            dma((heads,)),
        ],
        compiler_params=pltpu.CompilerParams(
            collective_id=0, has_side_effects=True, vmem_limit_bytes=GRANT
        ),
        cost_estimate=pl.CostEstimate(
            flops=5 * pairs * HEAD_DIM, bytes_accessed=10 * query_in.size, transcendentals=pairs
        ),
    )(span_place, query_in, key_in, value_in, out_saved, out_grad)
    shapes = (query_in.shape, key_in.shape, value_in.shape)
    return pl.pallas_call(
        sum_kernel,
        out_shape=tuple(jax.ShapeDtypeStruct(shape, low) for shape in shapes),
        in_specs=[hbm] * 2,
        out_specs=(hbm, hbm, hbm),
        scratch_shapes=[
            pltpu.VMEM(query_in.shape, low),
            pltpu.VMEM(pieces, low),
            pltpu.VMEM(key_in.shape, low),
            pltpu.VMEM(value_in.shape, low),
            dma((2,)),
            dma((3,)),
        ],
        compiler_params=pltpu.CompilerParams(vmem_limit_bytes=GRANT),
    )(*grads)


def solution(mesh):
    placed = (
        P(("ctx", "head"), None),
        P("ctx", "head"),
        P("ctx", "head"),
        P(("ctx", "head"), None),
        P(("ctx", "head"), None),
        P(),
    )
    return jax.shard_map(
        body,
        mesh=mesh,
        in_specs=placed,
        out_specs=(P(("ctx", "head"), None), P("ctx", "head"), P("ctx", "head")),
        check_vma=False,
    )
```

```python
import functools
import math

import jax
import jax.numpy as jnp
from jax import lax
from jax.experimental import pallas as pl
from jax.experimental.pallas import tpu as pltpu
from jax.sharding import PartitionSpec as P

HEAD_DIM = 128
CORES = 2
DELTA_ROWS = 16
GRANT = 56 * 1024 * 1024
MESH = pl.DeviceIdType.MESH
NT = (((1,), (1,)), ((), ()))
NN = (((1,), (0,)), ((), ()))


def matmul(a, b, dims):
    return lax.dot_general(a, b, dims, preferred_element_type=jnp.float32)


def columns(index):
    return pl.ds(pl.multiple_of(index * HEAD_DIM, HEAD_DIM), HEAD_DIM)


def kernel(
    ctx_size, head_size, place_in, query_in, key_in, value_in, saved_in, grad_in,
    dq_out, parts,
    qbuf, tbuf, kbuf, vbuf, key_cols, pbuf, dp_stage, dq_stage,
    own_grad, own_saved, token_src, place,
    send_sem, local_sem, q_sem, t_sem, k_sem, v_sem, p_sem, qp_sem,
):
    chips = ctx_size // CORES
    rows_high = max(chips // 2, 1)
    block = key_in.shape[0]
    token_rows = query_in.shape[0]
    heads = head_size * CORES
    rows = CORES * block
    span = ctx_size * block // place_in.shape[0]
    spans = rows // span
    scale = HEAD_DIM ** -0.5

    me = lax.axis_index("ctx")
    z = lax.axis_index("head")
    core = lax.rem(me, CORES)
    chip = me // CORES
    low, high = lax.rem(chip, 2), chip // 2

    def other_chip(step):
        return lax.rem(high + step // 2, rows_high) * 2 + lax.rem(low + step % 2, 2)

    def other_core(step):
        return lax.rem(core + step, CORES)

    def other_z(step):
        return lax.rem(z + step, head_size)

    chip_at = [other_chip(step) for step in range(chips)]
    core_at = [other_core(step) for step in range(CORES)]
    z_at = [other_z(step) for step in range(head_size)]
    plane = [(c, j) for c in range(chips) for j in range(CORES) if c or j]
    line = [(w, j) for w in range(head_size) for j in range(CORES) if w or j]

    def plane_id(c, j):
        return {"ctx": chip_at[c] * CORES + core_at[j], "head": z}

    def line_id(w, j):
        return {"ctx": chip * CORES + core_at[j], "head": z_at[w]}

    barrier = pltpu.get_barrier_semaphore()
    peers = [plane_id(c, j) for c, j in plane] + [line_id(w, j) for w, j in line if w]
    for peer in peers:
        pl.semaphore_signal(barrier, inc=1, device_id=peer, device_id_type=MESH)

    my_head = z * CORES + core
    held = ((grad_in, own_grad), (saved_in, own_saved), (place_in, place))
    loads = [pltpu.make_async_copy(src, dst, local_sem.at[i]) for i, (src, dst) in enumerate(held)]
    for load in loads:
        load.start()
    pltpu.make_async_copy(query_in.at[:, columns(my_head)], qbuf.at[core, z], q_sem.at[core, z]).start()
    pltpu.make_async_copy(key_in.at[:, columns(core)], kbuf.at[chip, core], k_sem.at[chip, core]).start()
    pltpu.make_async_copy(value_in.at[:, columns(core)], vbuf.at[chip, core], v_sem.at[chip, core]).start()

    pl.semaphore_wait(barrier, len(peers))

    sent = []

    def send(src, dst, sem, device):
        copy = pltpu.make_async_remote_copy(
            src_ref=src, dst_ref=dst, send_sem=send_sem.at[len(sent)], recv_sem=sem,
            device_id=device, device_id_type=MESH,
        )
        copy.start()
        sent.append(copy)

    def arrive(dst, sem):
        pltpu.make_async_copy(dst, dst, sem).wait()

    def send_plane(src, dst, sem):
        for c, j in plane[::-1]:
            send(src.at[:, columns(core_at[j])], dst.at[chip, core], sem.at[chip, core], plane_id(c, j))

    for w, j in line:
        src = query_in.at[:, columns(z_at[w] * CORES + core_at[j])]
        send(src, qbuf.at[core, z], q_sem.at[core, z], line_id(w, j))
    send_plane(key_in, kbuf, k_sem)
    send_plane(value_in, vbuf, v_sem)

    for load in loads:
        load.wait()
    product = own_grad[...].astype(jnp.float32) * own_saved[...].astype(jnp.float32)
    coarse = product.astype(jnp.bfloat16)
    fine = (product - coarse.astype(jnp.float32)).astype(jnp.bfloat16)
    shape = (heads, heads * HEAD_DIM)
    member = lax.broadcasted_iota(jnp.int32, shape, 1) // HEAD_DIM == lax.broadcasted_iota(jnp.int32, shape, 0)
    member = jnp.where(member, 1.0, 0.0).astype(jnp.bfloat16)
    delta = matmul(member, jnp.concatenate([coarse] * head_size, axis=0), NT)
    delta += matmul(member, jnp.concatenate([fine] * head_size, axis=0), NT)
    lane_z = lax.broadcasted_iota(jnp.int32, (heads, block), 1) // token_rows
    delta = jnp.where(lane_z == z, delta, 0.0)
    first = delta.astype(jnp.bfloat16).astype(jnp.float32)
    second = (delta - first).astype(jnp.bfloat16).astype(jnp.float32)
    third = delta - first - second
    padding = jnp.zeros((DELTA_ROWS - 3, block), jnp.float32)
    for h in range(heads):
        at = slice(h * HEAD_DIM, (h + 1) * HEAD_DIM)
        token_src[h, :token_rows] = own_grad[:, at]
        split = jnp.concatenate([first[h : h + 1], second[h : h + 1], third[h : h + 1], padding], axis=0)
        token_src[h, token_rows:] = split.astype(jnp.bfloat16)
    tbuf[core, z] = token_src[my_head]

    for w, j in line:
        send(token_src.at[z_at[w] * CORES + core_at[j]], tbuf.at[core, z], t_sem.at[core, z], line_id(w, j))

    lane = lax.broadcasted_iota(jnp.int32, (1, rows), 1)
    place_row = jnp.zeros((1, rows), jnp.int32)
    for s in range(spans):
        place_row = jnp.where(lane // span == s, place[chip * spans + s], place_row)
    pos_row = place_row * span + lane % span
    within = lax.broadcasted_iota(jnp.int32, (span, rows), 0)

    for j in range(CORES):
        for w in range(head_size):
            arrive(qbuf.at[j, w], q_sem.at[j, w])
    query = qbuf[...].reshape(rows, HEAD_DIM)
    query_cols = query.T

    def chunk(buf, c):
        return buf[chip_at[c]].reshape(rows, HEAD_DIM)

    tops, sums = [], []
    for c in range(chips):
        for j in range(CORES):
            arrive(kbuf.at[chip_at[c], j], k_sem.at[chip_at[c], j])
        keys = chunk(kbuf, c)
        key_cols[:, c * rows : (c + 1) * rows] = keys.T
        scores = matmul(keys, query_cols, NN) * (scale * math.log2(math.e))
        pieces = []
        for s in range(spans):
            limit = pos_row - place[chip_at[c] * spans + s] * span
            pieces.append(jnp.where(within <= limit, scores[s * span : (s + 1) * span], -1e30))
        masked = jnp.concatenate(pieces, axis=0)
        top = jnp.max(masked, axis=0, keepdims=True)
        probs = jnp.exp2(masked - top)
        pbuf[c] = probs
        tops.append(top)
        sums.append(jnp.sum(probs, axis=0, keepdims=True))

    best = functools.reduce(jnp.maximum, tops)
    weights = [jnp.exp2(top - best) for top in tops]
    total = functools.reduce(jnp.add, [w * s for w, s in zip(weights, sums)])
    weights = [w / total for w in weights]

    for w, j in line:
        arrive(tbuf.at[core_at[j], z_at[w]], t_sem.at[core_at[j], z_at[w]])
    grad = tbuf[:, :, :token_rows].reshape(rows, HEAD_DIM)
    delta_row = jnp.concatenate(
        [
            jnp.sum(
                functools.reduce(
                    jnp.add, [tbuf[j, w, token_rows :].astype(jnp.float32) for w in range(head_size)]
                ),
                axis=0, keepdims=True,
            )
            for j in range(CORES)
        ],
        axis=1,
    )

    grad_cols = grad.T

    def send_part(c, kind, total):
        total = total.astype(jnp.bfloat16)
        for j in range(CORES):
            dp_stage[c, j, kind] = total[j * block : (j + 1) * block]
        for j in range(CORES):
            src, dst = dp_stage.at[c, core_at[j], kind], parts.at[chip, core, kind]
            if c or j:
                send(src, dst, p_sem.at[kind, chip, core], plane_id(c, j))
            else:
                pltpu.make_async_copy(src, dst, p_sem.at[kind, chip, core]).start()

    far_first = list(range(chips))[::-1]
    for c in far_first:
        probs = pbuf[c] * weights[c]
        pbuf[c] = probs
        send_part(c, 1, matmul(probs.astype(jnp.bfloat16), grad, NN))

    grad_q = jnp.zeros((HEAD_DIM, rows), jnp.float32)
    for c in far_first[-1:] + far_first[:-1]:
        for j in range(CORES):
            arrive(vbuf.at[chip_at[c], j], v_sem.at[chip_at[c], j])
        dprobs = matmul(chunk(vbuf, c), grad_cols, NN)
        dscores = (pbuf[c] * (dprobs - delta_row) * scale).astype(jnp.bfloat16)
        send_part(c, 0, matmul(dscores, query, NN))
        grad_q += matmul(key_cols[:, c * rows : (c + 1) * rows], dscores, NN)
    grad_q = grad_q.T

    dq_stage[...] = grad_q.astype(jnp.bfloat16).reshape(dq_stage.shape)
    for w, j in line:
        dst = dq_out.at[:, columns(my_head)]
        send(dq_stage.at[core_at[j], z_at[w]], dst, qp_sem.at[my_head], line_id(w, j))
    own = pltpu.make_async_copy(dq_stage.at[core, z], dq_out.at[:, columns(my_head)], qp_sem.at[my_head])
    own.start()

    for c in range(chips):
        for j in range(CORES):
            for kind in range(2):
                arrive(parts.at[c, j, kind], p_sem.at[kind, c, j])
    for h in range(heads):
        arrive(dq_out.at[:, h * HEAD_DIM : (h + 1) * HEAD_DIM], qp_sem.at[h])
    for copy in sent:
        copy.wait_send()


def sum_kernel(dq, parts, dq_out, dk_out, dv_out, dq_buf, buf, dk_buf, dv_buf, load_sem, store_sem):
    chips, cores = parts.shape[:2]
    loads = [pltpu.make_async_copy(parts, buf, load_sem.at[0]), pltpu.make_async_copy(dq, dq_buf, load_sem.at[1])]
    for load in loads:
        load.start()
    loads[0].wait()
    stores = []
    for i, (total, out) in enumerate(((dk_buf, dk_out), (dv_buf, dv_out))):
        for j in range(cores):
            summed = buf[0, j, i].astype(jnp.float32)
            for c in range(1, chips):
                summed += buf[c, j, i].astype(jnp.float32)
            total[:, j * HEAD_DIM : (j + 1) * HEAD_DIM] = summed.astype(jnp.bfloat16)
        stores.append(pltpu.make_async_copy(total, out, store_sem.at[i]))
        stores[-1].start()
    loads[1].wait()
    stores.append(pltpu.make_async_copy(dq_buf, dq_out, store_sem.at[2]))
    stores[-1].start()
    for store in stores:
        store.wait()


def body(query_in, key_in, value_in, out_saved, out_grad, span_place):
    ctx_size, head_size = lax.axis_size("ctx"), lax.axis_size("head")
    chips = ctx_size // CORES
    block = key_in.shape[0]
    token_rows, width = query_in.shape
    heads = head_size * CORES
    rows = CORES * block
    low = jnp.bfloat16
    tokens = (CORES, head_size, token_rows, HEAD_DIM)
    message = (token_rows + DELTA_ROWS, HEAD_DIM)
    keys = (chips, CORES, block, HEAD_DIM)
    pieces = (chips, CORES, 2, block, HEAD_DIM)
    dma = pltpu.SemaphoreType.DMA
    copies = 4 * (ctx_size - 1) + 3 * (heads - 1)
    hbm = pl.BlockSpec(memory_space=pltpu.HBM)
    pairs = CORES * chips * rows * rows
    grads = pl.pallas_call(
        functools.partial(kernel, ctx_size, head_size),
        out_shape=(jax.ShapeDtypeStruct(query_in.shape, low), jax.ShapeDtypeStruct(pieces, low)),
        in_specs=[hbm] * 6,
        out_specs=(hbm, hbm),
        scratch_shapes=[
            pltpu.VMEM(tokens, low),
            pltpu.VMEM((CORES, head_size, *message), low),
            pltpu.VMEM(keys, low),
            pltpu.VMEM(keys, low),
            pltpu.VMEM((HEAD_DIM, chips * rows), low),
            pltpu.VMEM((chips, rows, rows), jnp.float32),
            pltpu.VMEM(pieces, low),
            pltpu.VMEM(tokens, low),
            pltpu.VMEM((token_rows, width), low),
            pltpu.VMEM((token_rows, width), low),
            pltpu.VMEM((heads, *message), low),
            pltpu.SMEM(span_place.shape, span_place.dtype),
            dma((copies,)),
            dma((3,)),
            dma((CORES, head_size)),
            dma((CORES, head_size)),
            dma((chips, CORES)),
            dma((chips, CORES)),
            dma((2, chips, CORES)),
            dma((heads,)),
        ],
        compiler_params=pltpu.CompilerParams(
            collective_id=0, has_side_effects=True, vmem_limit_bytes=GRANT
        ),
        cost_estimate=pl.CostEstimate(
            flops=5 * pairs * HEAD_DIM, bytes_accessed=10 * query_in.size, transcendentals=pairs
        ),
    )(span_place, query_in, key_in, value_in, out_saved, out_grad)
    shapes = (query_in.shape, key_in.shape, value_in.shape)
    return pl.pallas_call(
        sum_kernel,
        out_shape=tuple(jax.ShapeDtypeStruct(shape, low) for shape in shapes),
        in_specs=[hbm] * 2,
        out_specs=(hbm, hbm, hbm),
        scratch_shapes=[
            pltpu.VMEM(query_in.shape, low),
            pltpu.VMEM(pieces, low),
            pltpu.VMEM(key_in.shape, low),
            pltpu.VMEM(value_in.shape, low),
            dma((2,)),
            dma((3,)),
        ],
        compiler_params=pltpu.CompilerParams(vmem_limit_bytes=GRANT),
    )(*grads)


def solution(mesh):
    placed = (
        P(("ctx", "head"), None),
        P("ctx", "head"),
        P("ctx", "head"),
        P(("ctx", "head"), None),
        P(("ctx", "head"), None),
        P(),
    )
    return jax.shard_map(
        body,
        mesh=mesh,
        in_specs=placed,
        out_specs=(P(("ctx", "head"), None), P("ctx", "head"), P("ctx", "head")),
        check_vma=False,
    )
```

```python
import functools
import math

import jax
import jax.numpy as jnp
from jax import lax
from jax.experimental import pallas as pl
from jax.experimental.pallas import tpu as pltpu
from jax.sharding import PartitionSpec as P

HEAD_DIM = 128
CORES = 2
DELTA_ROWS = 16
GRANT = 56 * 1024 * 1024
SMALL_GRANT = 8 * 1024 * 1024
MESH = pl.DeviceIdType.MESH
NT = (((1,), (1,)), ((), ()))
NN = (((1,), (0,)), ((), ()))


def matmul(a, b, dims):
    return lax.dot_general(a, b, dims, preferred_element_type=jnp.float32)


def columns(index):
    return pl.ds(pl.multiple_of(index * HEAD_DIM, HEAD_DIM), HEAD_DIM)


def kernel(
    ctx_size, head_size, place_in, query_in, key_in, value_in, saved_in, grad_in,
    dq_out, parts,
    qbuf, tbuf, kbuf, vbuf, key_cols, pbuf, dp_stage, dq_stage,
    own_grad, own_saved, token_src, place,
    send_sem, local_sem, q_sem, t_sem, k_sem, v_sem, p_sem, qp_sem,
):
    chips = ctx_size // CORES
    rows_high = max(chips // 2, 1)
    block = key_in.shape[0]
    token_rows = query_in.shape[0]
    heads = head_size * CORES
    rows = CORES * block
    span = ctx_size * block // place_in.shape[0]
    spans = rows // span
    scale = HEAD_DIM ** -0.5

    me = lax.axis_index("ctx")
    z = lax.axis_index("head")
    core = lax.rem(me, CORES)
    chip = me // CORES
    low, high = lax.rem(chip, 2), chip // 2

    def other_chip(step):
        return lax.rem(high + step // 2, rows_high) * 2 + lax.rem(low + step % 2, 2)

    def other_core(step):
        return lax.rem(core + step, CORES)

    def other_z(step):
        return lax.rem(z + step, head_size)

    chip_at = [other_chip(step) for step in range(chips)]
    core_at = [other_core(step) for step in range(CORES)]
    z_at = [other_z(step) for step in range(head_size)]
    plane = [(c, j) for c in range(chips) for j in range(CORES) if c or j]
    line = [(w, j) for w in range(head_size) for j in range(CORES) if w or j]

    def plane_id(c, j):
        return {"ctx": chip_at[c] * CORES + core_at[j], "head": z}

    def line_id(w, j):
        return {"ctx": chip * CORES + core_at[j], "head": z_at[w]}

    barrier = pltpu.get_barrier_semaphore()
    peers = [plane_id(c, j) for c, j in plane] + [line_id(w, j) for w, j in line if w]
    for peer in peers:
        pl.semaphore_signal(barrier, inc=1, device_id=peer, device_id_type=MESH)

    my_head = z * CORES + core
    held = ((grad_in, own_grad), (saved_in, own_saved), (place_in, place))
    loads = [pltpu.make_async_copy(src, dst, local_sem.at[i]) for i, (src, dst) in enumerate(held)]
    for load in loads:
        load.start()
    pltpu.make_async_copy(query_in.at[:, columns(my_head)], qbuf.at[core, z], q_sem.at[core, z]).start()
    pltpu.make_async_copy(key_in.at[:, columns(core)], kbuf.at[chip, core], k_sem.at[chip, core]).start()
    pltpu.make_async_copy(value_in.at[:, columns(core)], vbuf.at[chip, core], v_sem.at[chip, core]).start()

    pl.semaphore_wait(barrier, len(peers))

    sent = []

    def send(src, dst, sem, device):
        copy = pltpu.make_async_remote_copy(
            src_ref=src, dst_ref=dst, send_sem=send_sem.at[len(sent)], recv_sem=sem,
            device_id=device, device_id_type=MESH,
        )
        copy.start()
        sent.append(copy)

    def arrive(dst, sem):
        pltpu.make_async_copy(dst, dst, sem).wait()

    def send_plane(src, dst, sem):
        for c, j in plane[::-1]:
            send(src.at[:, columns(core_at[j])], dst.at[chip, core], sem.at[chip, core], plane_id(c, j))

    for w, j in line:
        src = query_in.at[:, columns(z_at[w] * CORES + core_at[j])]
        send(src, qbuf.at[core, z], q_sem.at[core, z], line_id(w, j))
    send_plane(key_in, kbuf, k_sem)
    send_plane(value_in, vbuf, v_sem)

    for load in loads:
        load.wait()
    product = own_grad[...].astype(jnp.float32) * own_saved[...].astype(jnp.float32)
    coarse = product.astype(jnp.bfloat16)
    fine = (product - coarse.astype(jnp.float32)).astype(jnp.bfloat16)
    shape = (heads, heads * HEAD_DIM)
    member = lax.broadcasted_iota(jnp.int32, shape, 1) // HEAD_DIM == lax.broadcasted_iota(jnp.int32, shape, 0)
    member = jnp.where(member, 1.0, 0.0).astype(jnp.bfloat16)
    delta = matmul(member, jnp.concatenate([coarse] * head_size, axis=0), NT)
    delta += matmul(member, jnp.concatenate([fine] * head_size, axis=0), NT)
    lane_z = lax.broadcasted_iota(jnp.int32, (heads, block), 1) // token_rows
    delta = jnp.where(lane_z == z, delta, 0.0)
    first = delta.astype(jnp.bfloat16).astype(jnp.float32)
    second = (delta - first).astype(jnp.bfloat16).astype(jnp.float32)
    third = delta - first - second
    padding = jnp.zeros((DELTA_ROWS - 3, block), jnp.float32)
    for h in range(heads):
        at = slice(h * HEAD_DIM, (h + 1) * HEAD_DIM)
        token_src[h, :token_rows] = own_grad[:, at]
        split = jnp.concatenate([first[h : h + 1], second[h : h + 1], third[h : h + 1], padding], axis=0)
        token_src[h, token_rows:] = split.astype(jnp.bfloat16)
    tbuf[core, z] = token_src[my_head]

    for w, j in line:
        send(token_src.at[z_at[w] * CORES + core_at[j]], tbuf.at[core, z], t_sem.at[core, z], line_id(w, j))

    lane = lax.broadcasted_iota(jnp.int32, (1, rows), 1)
    place_row = jnp.zeros((1, rows), jnp.int32)
    for s in range(spans):
        place_row = jnp.where(lane // span == s, place[chip * spans + s], place_row)
    pos_row = place_row * span + lane % span
    within = lax.broadcasted_iota(jnp.int32, (span, rows), 0)

    for j in range(CORES):
        for w in range(head_size):
            arrive(qbuf.at[j, w], q_sem.at[j, w])
    query = qbuf[...].reshape(rows, HEAD_DIM)
    query_cols = query.T

    def chunk(buf, c):
        return buf[chip_at[c]].reshape(rows, HEAD_DIM)

    tops, sums = [], []
    for c in range(chips):
        for j in range(CORES):
            arrive(kbuf.at[chip_at[c], j], k_sem.at[chip_at[c], j])
        keys = chunk(kbuf, c)
        key_cols[:, c * rows : (c + 1) * rows] = keys.T
        scores = matmul(keys, query_cols, NN) * (scale * math.log2(math.e))
        pieces = []
        for s in range(spans):
            limit = pos_row - place[chip_at[c] * spans + s] * span
            pieces.append(jnp.where(within <= limit, scores[s * span : (s + 1) * span], -1e30))
        masked = jnp.concatenate(pieces, axis=0)
        top = jnp.max(masked, axis=0, keepdims=True)
        probs = jnp.exp2(masked - top)
        pbuf[c] = probs
        tops.append(top)
        sums.append(jnp.sum(probs, axis=0, keepdims=True))

    best = functools.reduce(jnp.maximum, tops)
    weights = [jnp.exp2(top - best) for top in tops]
    total = functools.reduce(jnp.add, [w * s for w, s in zip(weights, sums)])
    weights = [w / total for w in weights]

    for w, j in line:
        arrive(tbuf.at[core_at[j], z_at[w]], t_sem.at[core_at[j], z_at[w]])
    grad = tbuf[:, :, :token_rows].reshape(rows, HEAD_DIM)
    delta_row = jnp.concatenate(
        [
            jnp.sum(
                functools.reduce(
                    jnp.add, [tbuf[j, w, token_rows :].astype(jnp.float32) for w in range(head_size)]
                ),
                axis=0, keepdims=True,
            )
            for j in range(CORES)
        ],
        axis=1,
    )

    grad_cols = grad.T

    def send_part(c, kind, total):
        total = total.astype(jnp.bfloat16)
        for j in range(CORES):
            dp_stage[c, j, kind] = total[j * block : (j + 1) * block]
        for j in range(CORES):
            src, dst = dp_stage.at[c, core_at[j], kind], parts.at[chip, core, kind]
            if c or j:
                send(src, dst, p_sem.at[kind, chip, core], plane_id(c, j))
            else:
                pltpu.make_async_copy(src, dst, p_sem.at[kind, chip, core]).start()

    far_first = list(range(chips))[::-1]
    for c in far_first:
        probs = pbuf[c] * weights[c]
        pbuf[c] = probs
        send_part(c, 1, matmul(probs.astype(jnp.bfloat16), grad, NN))

    grad_q = jnp.zeros((HEAD_DIM, rows), jnp.float32)
    for c in far_first[-1:] + far_first[:-1]:
        for j in range(CORES):
            arrive(vbuf.at[chip_at[c], j], v_sem.at[chip_at[c], j])
        dprobs = matmul(chunk(vbuf, c), grad_cols, NN)
        dscores = (pbuf[c] * (dprobs - delta_row) * scale).astype(jnp.bfloat16)
        send_part(c, 0, matmul(dscores, query, NN))
        grad_q += matmul(key_cols[:, c * rows : (c + 1) * rows], dscores, NN)
    grad_q = grad_q.T

    dq_stage[...] = grad_q.astype(jnp.bfloat16).reshape(dq_stage.shape)
    for w, j in line:
        dst = dq_out.at[:, columns(my_head)]
        send(dq_stage.at[core_at[j], z_at[w]], dst, qp_sem.at[my_head], line_id(w, j))
    own = pltpu.make_async_copy(dq_stage.at[core, z], dq_out.at[:, columns(my_head)], qp_sem.at[my_head])
    own.start()

    for c in range(chips):
        for j in range(CORES):
            for kind in range(2):
                arrive(parts.at[c, j, kind], p_sem.at[kind, c, j])
    for h in range(heads):
        arrive(dq_out.at[:, h * HEAD_DIM : (h + 1) * HEAD_DIM], qp_sem.at[h])
    for copy in sent:
        copy.wait_send()


def sum_kernel(dq, parts, dq_out, dk_out, dv_out, dk_buf, dv_buf, store_sem):
    chips, cores = parts.shape[:2]
    stores = [pltpu.make_async_copy(dq, dq_out, store_sem.at[2])]
    stores[0].start()
    for i, (total, out) in enumerate(((dk_buf, dk_out), (dv_buf, dv_out))):
        for j in range(cores):
            summed = parts[0, j, i].astype(jnp.float32)
            for c in range(1, chips):
                summed += parts[c, j, i].astype(jnp.float32)
            total[:, j * HEAD_DIM : (j + 1) * HEAD_DIM] = summed.astype(jnp.bfloat16)
        stores.append(pltpu.make_async_copy(total, out, store_sem.at[i]))
        stores[-1].start()
    for store in stores:
        store.wait()


def body(query_in, key_in, value_in, out_saved, out_grad, span_place):
    ctx_size, head_size = lax.axis_size("ctx"), lax.axis_size("head")
    chips = ctx_size // CORES
    block = key_in.shape[0]
    token_rows, width = query_in.shape
    heads = head_size * CORES
    rows = CORES * block
    low = jnp.bfloat16
    tokens = (CORES, head_size, token_rows, HEAD_DIM)
    message = (token_rows + DELTA_ROWS, HEAD_DIM)
    keys = (chips, CORES, block, HEAD_DIM)
    pieces = (chips, CORES, 2, block, HEAD_DIM)
    dma = pltpu.SemaphoreType.DMA
    copies = 4 * (ctx_size - 1) + 3 * (heads - 1)
    hbm = pl.BlockSpec(memory_space=pltpu.HBM)
    vmem = pl.BlockSpec(memory_space=pltpu.VMEM)
    pairs = CORES * chips * rows * rows
    grads = pl.pallas_call(
        functools.partial(kernel, ctx_size, head_size),
        out_shape=(pltpu.VMEM(query_in.shape, low), pltpu.VMEM(pieces, low)),
        in_specs=[hbm] * 6,
        out_specs=(vmem, vmem),
        scratch_shapes=[
            pltpu.VMEM(tokens, low),
            pltpu.VMEM((CORES, head_size, *message), low),
            pltpu.VMEM(keys, low),
            pltpu.VMEM(keys, low),
            pltpu.VMEM((HEAD_DIM, chips * rows), low),
            pltpu.VMEM((chips, rows, rows), jnp.float32),
            pltpu.VMEM(pieces, low),
            pltpu.VMEM(tokens, low),
            pltpu.VMEM((token_rows, width), low),
            pltpu.VMEM((token_rows, width), low),
            pltpu.VMEM((heads, *message), low),
            pltpu.SMEM(span_place.shape, span_place.dtype),
            dma((copies,)),
            dma((3,)),
            dma((CORES, head_size)),
            dma((CORES, head_size)),
            dma((chips, CORES)),
            dma((chips, CORES)),
            dma((2, chips, CORES)),
            dma((heads,)),
        ],
        compiler_params=pltpu.CompilerParams(
            collective_id=0, has_side_effects=True, vmem_limit_bytes=GRANT
        ),
        cost_estimate=pl.CostEstimate(
            flops=5 * pairs * HEAD_DIM, bytes_accessed=10 * query_in.size, transcendentals=pairs
        ),
    )(span_place, query_in, key_in, value_in, out_saved, out_grad)
    shapes = (query_in.shape, key_in.shape, value_in.shape)
    return pl.pallas_call(
        sum_kernel,
        out_shape=tuple(jax.ShapeDtypeStruct(shape, low) for shape in shapes),
        in_specs=[vmem] * 2,
        out_specs=(hbm, hbm, hbm),
        scratch_shapes=[
            pltpu.VMEM(key_in.shape, low),
            pltpu.VMEM(value_in.shape, low),
            dma((3,)),
        ],
        compiler_params=pltpu.CompilerParams(vmem_limit_bytes=SMALL_GRANT),
    )(*grads)


def solution(mesh):
    placed = (
        P(("ctx", "head"), None),
        P("ctx", "head"),
        P("ctx", "head"),
        P(("ctx", "head"), None),
        P(("ctx", "head"), None),
        P(),
    )
    return jax.shard_map(
        body,
        mesh=mesh,
        in_specs=placed,
        out_specs=(P(("ctx", "head"), None), P("ctx", "head"), P("ctx", "head")),
        check_vma=False,
    )
```

```python
import functools
import math

import jax
import jax.numpy as jnp
from jax import lax
from jax.experimental import pallas as pl
from jax.experimental.pallas import tpu as pltpu
from jax.sharding import PartitionSpec as P

HEAD_DIM = 128
CORES = 2
DELTA_ROWS = 16
GRANT = 56 * 1024 * 1024
SMALL_GRANT = 8 * 1024 * 1024
MESH = pl.DeviceIdType.MESH
NT = (((1,), (1,)), ((), ()))
NN = (((1,), (0,)), ((), ()))


def matmul(a, b, dims):
    return lax.dot_general(a, b, dims, preferred_element_type=jnp.float32)


def columns(index):
    return pl.ds(pl.multiple_of(index * HEAD_DIM, HEAD_DIM), HEAD_DIM)


def kernel(
    ctx_size, head_size, place_in, query_in, key_in, value_in, saved_in, grad_in,
    dq_out, parts,
    qbuf, tbuf, kbuf, vbuf, key_cols, pbuf, dp_stage, dq_stage,
    own_grad, own_saved, token_src, place,
    send_sem, local_sem, q_sem, t_sem, k_sem, v_sem, p_sem, qp_sem,
):
    chips = ctx_size // CORES
    rows_high = max(chips // 2, 1)
    block = key_in.shape[0]
    token_rows = query_in.shape[0]
    heads = head_size * CORES
    rows = CORES * block
    span = ctx_size * block // place_in.shape[0]
    spans = rows // span
    scale = HEAD_DIM ** -0.5

    me = lax.axis_index("ctx")
    z = lax.axis_index("head")
    core = lax.rem(me, CORES)
    chip = me // CORES
    low, high = lax.rem(chip, 2), chip // 2

    def other_chip(step):
        return lax.rem(high + step // 2, rows_high) * 2 + lax.rem(low + step % 2, 2)

    def other_core(step):
        return lax.rem(core + step, CORES)

    def other_z(step):
        return lax.rem(z + step, head_size)

    chip_at = [other_chip(step) for step in range(chips)]
    core_at = [other_core(step) for step in range(CORES)]
    z_at = [other_z(step) for step in range(head_size)]
    plane = [(c, j) for c in range(chips) for j in range(CORES) if c or j]
    line = [(w, j) for w in range(head_size) for j in range(CORES) if w or j]

    def plane_id(c, j):
        return {"ctx": chip_at[c] * CORES + core_at[j], "head": z}

    def line_id(w, j):
        return {"ctx": chip * CORES + core_at[j], "head": z_at[w]}

    barrier = pltpu.get_barrier_semaphore()
    peers = [plane_id(c, j) for c, j in plane] + [line_id(w, j) for w, j in line if w]
    for peer in peers:
        pl.semaphore_signal(barrier, inc=1, device_id=peer, device_id_type=MESH)

    my_head = z * CORES + core
    held = ((grad_in, own_grad), (saved_in, own_saved), (place_in, place))
    loads = [pltpu.make_async_copy(src, dst, local_sem.at[i]) for i, (src, dst) in enumerate(held)]
    for load in loads:
        load.start()
    pltpu.make_async_copy(query_in.at[:, columns(my_head)], qbuf.at[core, z], q_sem.at[0]).start()
    pltpu.make_async_copy(key_in.at[:, columns(core)], kbuf.at[chip, core], k_sem.at[chip]).start()
    pltpu.make_async_copy(value_in.at[:, columns(core)], vbuf.at[chip, core], v_sem.at[chip]).start()

    pl.semaphore_wait(barrier, len(peers))

    sent = []

    def send(src, dst, sem, device):
        copy = pltpu.make_async_remote_copy(
            src_ref=src, dst_ref=dst, send_sem=send_sem.at[len(sent)], recv_sem=sem,
            device_id=device, device_id_type=MESH,
        )
        copy.start()
        sent.append(copy)

    def arrive(dst, sem):
        pltpu.make_async_copy(dst, dst, sem).wait()

    def send_plane(src, dst, sem):
        for c, j in plane[::-1]:
            send(src.at[:, columns(core_at[j])], dst.at[chip, core], sem.at[chip], plane_id(c, j))

    for w, j in line:
        src = query_in.at[:, columns(z_at[w] * CORES + core_at[j])]
        send(src, qbuf.at[core, z], q_sem.at[0], line_id(w, j))
    send_plane(key_in, kbuf, k_sem)

    for load in loads:
        load.wait()
    product = own_grad[...].astype(jnp.float32) * own_saved[...].astype(jnp.float32)
    coarse = product.astype(jnp.bfloat16)
    fine = (product - coarse.astype(jnp.float32)).astype(jnp.bfloat16)
    shape = (heads, heads * HEAD_DIM)
    member = lax.broadcasted_iota(jnp.int32, shape, 1) // HEAD_DIM == lax.broadcasted_iota(jnp.int32, shape, 0)
    member = jnp.where(member, 1.0, 0.0).astype(jnp.bfloat16)
    delta = matmul(member, jnp.concatenate([coarse] * head_size, axis=0), NT)
    delta += matmul(member, jnp.concatenate([fine] * head_size, axis=0), NT)
    lane_z = lax.broadcasted_iota(jnp.int32, (heads, block), 1) // token_rows
    delta = jnp.where(lane_z == z, delta, 0.0)
    first = delta.astype(jnp.bfloat16).astype(jnp.float32)
    second = (delta - first).astype(jnp.bfloat16).astype(jnp.float32)
    third = delta - first - second
    padding = jnp.zeros((DELTA_ROWS - 3, block), jnp.float32)
    for h in range(heads):
        at = slice(h * HEAD_DIM, (h + 1) * HEAD_DIM)
        token_src[h, :token_rows] = own_grad[:, at]
        split = jnp.concatenate([first[h : h + 1], second[h : h + 1], third[h : h + 1], padding], axis=0)
        token_src[h, token_rows:] = split.astype(jnp.bfloat16)
    pltpu.make_async_copy(token_src.at[my_head], tbuf.at[core, z], t_sem.at[0]).start()

    for w, j in line:
        send(token_src.at[z_at[w] * CORES + core_at[j]], tbuf.at[core, z], t_sem.at[0], line_id(w, j))
    send_plane(value_in, vbuf, v_sem)

    lane = lax.broadcasted_iota(jnp.int32, (1, rows), 1)
    place_row = jnp.zeros((1, rows), jnp.int32)
    for s in range(spans):
        place_row = jnp.where(lane // span == s, place[chip * spans + s], place_row)
    pos_row = place_row * span + lane % span
    within = lax.broadcasted_iota(jnp.int32, (span, rows), 0)

    arrive(qbuf, q_sem.at[0])
    query = qbuf[...].reshape(rows, HEAD_DIM)
    query_cols = query.T

    def chunk(buf, c):
        return buf[chip_at[c]].reshape(rows, HEAD_DIM)

    tops, sums = [], []
    for c in range(chips):
        arrive(kbuf.at[chip_at[c]], k_sem.at[chip_at[c]])
        keys = chunk(kbuf, c)
        key_cols[:, c * rows : (c + 1) * rows] = keys.T
        scores = matmul(keys, query_cols, NN) * (scale * math.log2(math.e))
        pieces = []
        for s in range(spans):
            limit = pos_row - place[chip_at[c] * spans + s] * span
            pieces.append(jnp.where(within <= limit, scores[s * span : (s + 1) * span], -1e30))
        masked = jnp.concatenate(pieces, axis=0)
        top = jnp.max(masked, axis=0, keepdims=True)
        probs = jnp.exp2(masked - top)
        pbuf[c] = probs
        tops.append(top)
        sums.append(jnp.sum(probs, axis=0, keepdims=True))

    best = functools.reduce(jnp.maximum, tops)
    weights = [jnp.exp2(top - best) for top in tops]
    total = functools.reduce(jnp.add, [w * s for w, s in zip(weights, sums)])
    weights = [w / total for w in weights]

    arrive(tbuf, t_sem.at[0])
    grad = tbuf[:, :, :token_rows].reshape(rows, HEAD_DIM)
    delta_row = jnp.concatenate(
        [
            jnp.sum(
                functools.reduce(
                    jnp.add, [tbuf[j, w, token_rows :].astype(jnp.float32) for w in range(head_size)]
                ),
                axis=0, keepdims=True,
            )
            for j in range(CORES)
        ],
        axis=1,
    )

    grad_cols = grad.T

    def send_part(c, kind, total):
        total = total.astype(jnp.bfloat16)
        for j in range(CORES):
            dp_stage[c, j, kind] = total[j * block : (j + 1) * block]
        for j in range(CORES):
            src, dst = dp_stage.at[c, core_at[j], kind], parts.at[chip, core, kind]
            if c or j:
                send(src, dst, p_sem.at[0], plane_id(c, j))
            else:
                pltpu.make_async_copy(src, dst, p_sem.at[0]).start()

    far_first = list(range(chips))[::-1]
    for c in far_first:
        probs = pbuf[c] * weights[c]
        pbuf[c] = probs
        send_part(c, 1, matmul(probs.astype(jnp.bfloat16), grad, NN))

    grad_q = jnp.zeros((HEAD_DIM, rows), jnp.float32)
    order = far_first[-1:] + far_first[:-1]
    last = order[-1]
    for c in order:
        arrive(vbuf.at[chip_at[c]], v_sem.at[chip_at[c]])
        dprobs = matmul(chunk(vbuf, c), grad_cols, NN)
        dscores = (pbuf[c] * (dprobs - delta_row) * scale).astype(jnp.bfloat16)
        grad_q += matmul(key_cols[:, c * rows : (c + 1) * rows], dscores, NN)
        if c == last:
            dq_stage[...] = grad_q.T.astype(jnp.bfloat16).reshape(dq_stage.shape)
            dst = dq_out.at[:, columns(my_head)]
            for w, j in line:
                send(dq_stage.at[core_at[j], z_at[w]], dst, qp_sem.at[0], line_id(w, j))
            pltpu.make_async_copy(dq_stage.at[core, z], dst, qp_sem.at[0]).start()
        send_part(c, 0, matmul(dscores, query, NN))

    for copy in sent:
        copy.wait_send()
    arrive(dq_out, qp_sem.at[0])
    arrive(parts, p_sem.at[0])


def sum_kernel(dq, parts, dq_out, dk_out, dv_out, dk_buf, dv_buf, store_sem):
    chips, cores = parts.shape[:2]
    stores = [pltpu.make_async_copy(dq, dq_out, store_sem.at[2])]
    stores[0].start()
    for i, (total, out) in enumerate(((dk_buf, dk_out), (dv_buf, dv_out))):
        for j in range(cores):
            summed = parts[0, j, i].astype(jnp.float32)
            for c in range(1, chips):
                summed += parts[c, j, i].astype(jnp.float32)
            total[:, j * HEAD_DIM : (j + 1) * HEAD_DIM] = summed.astype(jnp.bfloat16)
        stores.append(pltpu.make_async_copy(total, out, store_sem.at[i]))
        stores[-1].start()
    for store in stores:
        store.wait()


def body(query_in, key_in, value_in, out_saved, out_grad, span_place):
    ctx_size, head_size = lax.axis_size("ctx"), lax.axis_size("head")
    chips = ctx_size // CORES
    block = key_in.shape[0]
    token_rows, width = query_in.shape
    heads = head_size * CORES
    rows = CORES * block
    low = jnp.bfloat16
    tokens = (CORES, head_size, token_rows, HEAD_DIM)
    message = (token_rows + DELTA_ROWS, HEAD_DIM)
    keys = (chips, CORES, block, HEAD_DIM)
    pieces = (chips, CORES, 2, block, HEAD_DIM)
    dma = pltpu.SemaphoreType.DMA
    copies = 4 * (ctx_size - 1) + 3 * (heads - 1)
    hbm = pl.BlockSpec(memory_space=pltpu.HBM)
    vmem = pl.BlockSpec(memory_space=pltpu.VMEM)
    pairs = CORES * chips * rows * rows
    grads = pl.pallas_call(
        functools.partial(kernel, ctx_size, head_size),
        out_shape=(pltpu.VMEM(query_in.shape, low), pltpu.VMEM(pieces, low)),
        in_specs=[hbm] * 6,
        out_specs=(vmem, vmem),
        scratch_shapes=[
            pltpu.VMEM(tokens, low),
            pltpu.VMEM((CORES, head_size, *message), low),
            pltpu.VMEM(keys, low),
            pltpu.VMEM(keys, low),
            pltpu.VMEM((HEAD_DIM, chips * rows), low),
            pltpu.VMEM((chips, rows, rows), jnp.float32),
            pltpu.VMEM(pieces, low),
            pltpu.VMEM(tokens, low),
            pltpu.VMEM((token_rows, width), low),
            pltpu.VMEM((token_rows, width), low),
            pltpu.VMEM((heads, *message), low),
            pltpu.SMEM(span_place.shape, span_place.dtype),
            dma((copies,)),
            dma((3,)),
            dma((1,)),
            dma((1,)),
            dma((chips,)),
            dma((chips,)),
            dma((1,)),
            dma((1,)),
        ],
        compiler_params=pltpu.CompilerParams(
            collective_id=0, has_side_effects=True, vmem_limit_bytes=GRANT
        ),
        cost_estimate=pl.CostEstimate(
            flops=5 * pairs * HEAD_DIM, bytes_accessed=10 * query_in.size, transcendentals=pairs
        ),
    )(span_place, query_in, key_in, value_in, out_saved, out_grad)
    shapes = (query_in.shape, key_in.shape, value_in.shape)
    return pl.pallas_call(
        sum_kernel,
        out_shape=tuple(jax.ShapeDtypeStruct(shape, low) for shape in shapes),
        in_specs=[vmem] * 2,
        out_specs=(hbm, hbm, hbm),
        scratch_shapes=[
            pltpu.VMEM(key_in.shape, low),
            pltpu.VMEM(value_in.shape, low),
            dma((3,)),
        ],
        compiler_params=pltpu.CompilerParams(vmem_limit_bytes=SMALL_GRANT),
    )(*grads)


def solution(mesh):
    placed = (
        P(("ctx", "head"), None),
        P("ctx", "head"),
        P("ctx", "head"),
        P(("ctx", "head"), None),
        P(("ctx", "head"), None),
        P(),
    )
    return jax.shard_map(
        body,
        mesh=mesh,
        in_specs=placed,
        out_specs=(P(("ctx", "head"), None), P("ctx", "head"), P("ctx", "head")),
        check_vma=False,
    )
```

```python
import functools
import math

import jax
import jax.numpy as jnp
from jax import lax
from jax.experimental import pallas as pl
from jax.experimental.pallas import tpu as pltpu
from jax.sharding import PartitionSpec as P

HEAD_DIM = 128
CORES = 2
DELTA_ROWS = 16
GRANT = 56 * 1024 * 1024
SMALL_GRANT = 8 * 1024 * 1024
MESH = pl.DeviceIdType.MESH
NT = (((1,), (1,)), ((), ()))
NN = (((1,), (0,)), ((), ()))


def matmul(a, b, dims):
    return lax.dot_general(a, b, dims, preferred_element_type=jnp.float32)


def columns(index):
    return pl.ds(pl.multiple_of(index * HEAD_DIM, HEAD_DIM), HEAD_DIM)


def kernel(
    ctx_size, head_size, place_in, query_in, key_in, value_in, saved_in, grad_in,
    dq_out, parts,
    qbuf, tbuf, kbuf, vbuf, key_cols, pbuf, dp_stage, dq_stage,
    own_grad, own_saved, token_src, place,
    send_sem, local_sem, q_sem, t_sem, k_sem, v_sem, p_sem, qp_sem,
):
    chips = ctx_size // CORES
    rows_high = max(chips // 2, 1)
    block = key_in.shape[0]
    token_rows = query_in.shape[0]
    heads = head_size * CORES
    rows = CORES * block
    span = ctx_size * block // place_in.shape[0]
    spans = rows // span
    scale = HEAD_DIM ** -0.5

    me = lax.axis_index("ctx")
    z = lax.axis_index("head")
    core = lax.rem(me, CORES)
    chip = me // CORES
    low, high = lax.rem(chip, 2), chip // 2

    def other_chip(step):
        return lax.rem(high + step // 2, rows_high) * 2 + lax.rem(low + step % 2, 2)

    def other_core(step):
        return lax.rem(core + step, CORES)

    def other_z(step):
        return lax.rem(z + step, head_size)

    chip_at = [other_chip(step) for step in range(chips)]
    core_at = [other_core(step) for step in range(CORES)]
    z_at = [other_z(step) for step in range(head_size)]
    plane = [(c, j) for c in range(chips) for j in range(CORES) if c or j][::-1]
    line = [(w, j) for w in range(head_size) for j in range(CORES) if w or j][::-1]

    def plane_id(c, j):
        return {"ctx": chip_at[c] * CORES + core_at[j], "head": z}

    def line_id(w, j):
        return {"ctx": chip * CORES + core_at[j], "head": z_at[w]}

    barrier = pltpu.get_barrier_semaphore()
    peers = [line_id(w, j) for w, j in line if w] + [plane_id(c, j) for c, j in plane]
    for peer in peers:
        pl.semaphore_signal(barrier, inc=1, device_id=peer, device_id_type=MESH)

    my_head = z * CORES + core
    held = ((grad_in, own_grad), (saved_in, own_saved), (place_in, place))
    loads = [pltpu.make_async_copy(src, dst, local_sem.at[i]) for i, (src, dst) in enumerate(held)]
    for load in loads:
        load.start()
    pltpu.make_async_copy(query_in.at[:, columns(my_head)], qbuf.at[core, z], q_sem.at[0]).start()
    pltpu.make_async_copy(key_in.at[:, columns(core)], kbuf.at[chip, core], k_sem.at[chip]).start()
    pltpu.make_async_copy(value_in.at[:, columns(core)], vbuf.at[chip, core], v_sem.at[chip]).start()

    pl.semaphore_wait(barrier, len(peers))

    sent = []

    def send(src, dst, sem, device):
        copy = pltpu.make_async_remote_copy(
            src_ref=src, dst_ref=dst, send_sem=send_sem.at[len(sent)], recv_sem=sem,
            device_id=device, device_id_type=MESH,
        )
        copy.start()
        sent.append(copy)

    def arrive(dst, sem):
        pltpu.make_async_copy(dst, dst, sem).wait()

    def send_plane(src, dst, sem):
        for c, j in plane:
            send(src.at[:, columns(core_at[j])], dst.at[chip, core], sem.at[chip], plane_id(c, j))

    for w, j in line:
        src = query_in.at[:, columns(z_at[w] * CORES + core_at[j])]
        send(src, qbuf.at[core, z], q_sem.at[0], line_id(w, j))
    send_plane(key_in, kbuf, k_sem)

    for load in loads:
        load.wait()
    product = own_grad[...].astype(jnp.float32) * own_saved[...].astype(jnp.float32)
    coarse = product.astype(jnp.bfloat16)
    fine = (product - coarse.astype(jnp.float32)).astype(jnp.bfloat16)
    shape = (heads, heads * HEAD_DIM)
    member = lax.broadcasted_iota(jnp.int32, shape, 1) // HEAD_DIM == lax.broadcasted_iota(jnp.int32, shape, 0)
    member = jnp.where(member, 1.0, 0.0).astype(jnp.bfloat16)
    delta = matmul(member, jnp.concatenate([coarse] * head_size, axis=0), NT)
    delta += matmul(member, jnp.concatenate([fine] * head_size, axis=0), NT)
    lane_z = lax.broadcasted_iota(jnp.int32, (heads, block), 1) // token_rows
    delta = jnp.where(lane_z == z, delta, 0.0)
    first = delta.astype(jnp.bfloat16).astype(jnp.float32)
    second = (delta - first).astype(jnp.bfloat16).astype(jnp.float32)
    third = delta - first - second
    padding = jnp.zeros((DELTA_ROWS - 3, block), jnp.float32)
    for h in range(heads):
        at = slice(h * HEAD_DIM, (h + 1) * HEAD_DIM)
        token_src[h, :token_rows] = own_grad[:, at]
        split = jnp.concatenate([first[h : h + 1], second[h : h + 1], third[h : h + 1], padding], axis=0)
        token_src[h, token_rows:] = split.astype(jnp.bfloat16)
    pltpu.make_async_copy(token_src.at[my_head], tbuf.at[core, z], t_sem.at[0]).start()

    for w, j in line:
        send(token_src.at[z_at[w] * CORES + core_at[j]], tbuf.at[core, z], t_sem.at[0], line_id(w, j))
    send_plane(value_in, vbuf, v_sem)

    lane = lax.broadcasted_iota(jnp.int32, (1, rows), 1)
    place_row = jnp.zeros((1, rows), jnp.int32)
    for s in range(spans):
        place_row = jnp.where(lane // span == s, place[chip * spans + s], place_row)
    pos_row = place_row * span + lane % span
    within = lax.broadcasted_iota(jnp.int32, (span, rows), 0)

    arrive(qbuf, q_sem.at[0])
    query = qbuf[...].reshape(rows, HEAD_DIM)
    query_cols = query.T

    def chunk(buf, c):
        return buf[chip_at[c]].reshape(rows, HEAD_DIM)

    tops, sums = [], []
    for c in range(chips):
        arrive(kbuf.at[chip_at[c]], k_sem.at[chip_at[c]])
        keys = chunk(kbuf, c)
        key_cols[:, c * rows : (c + 1) * rows] = keys.T
        scores = matmul(keys, query_cols, NN) * (scale * math.log2(math.e))
        pieces = []
        for s in range(spans):
            limit = pos_row - place[chip_at[c] * spans + s] * span
            pieces.append(jnp.where(within <= limit, scores[s * span : (s + 1) * span], -1e30))
        masked = jnp.concatenate(pieces, axis=0)
        top = jnp.max(masked, axis=0, keepdims=True)
        probs = jnp.exp2(masked - top)
        pbuf[c] = probs
        tops.append(top)
        sums.append(jnp.sum(probs, axis=0, keepdims=True))

    best = functools.reduce(jnp.maximum, tops)
    weights = [jnp.exp2(top - best) for top in tops]
    total = functools.reduce(jnp.add, [w * s for w, s in zip(weights, sums)])
    weights = [w / total for w in weights]

    arrive(tbuf, t_sem.at[0])
    grad = tbuf[:, :, :token_rows].reshape(rows, HEAD_DIM)
    delta_row = jnp.concatenate(
        [
            jnp.sum(
                functools.reduce(
                    jnp.add, [tbuf[j, w, token_rows :].astype(jnp.float32) for w in range(head_size)]
                ),
                axis=0, keepdims=True,
            )
            for j in range(CORES)
        ],
        axis=1,
    )

    grad_cols = grad.T

    def send_part(c, kind, total):
        total = total.astype(jnp.bfloat16)
        for j in range(CORES):
            dp_stage[c, j, kind] = total[j * block : (j + 1) * block]
        for j in range(CORES):
            src, dst = dp_stage.at[c, core_at[j], kind], parts.at[chip, core, kind]
            if c or j:
                send(src, dst, p_sem.at[0], plane_id(c, j))
            else:
                pltpu.make_async_copy(src, dst, p_sem.at[0]).start()

    far_first = list(range(chips))[::-1]
    for c in far_first:
        probs = pbuf[c] * weights[c]
        pbuf[c] = probs
        send_part(c, 1, matmul(probs.astype(jnp.bfloat16), grad, NN))

    grad_q = jnp.zeros((HEAD_DIM, rows), jnp.float32)
    for c in far_first:
        arrive(vbuf.at[chip_at[c]], v_sem.at[chip_at[c]])
        dprobs = matmul(chunk(vbuf, c), grad_cols, NN)
        dscores = (pbuf[c] * (dprobs - delta_row) * scale).astype(jnp.bfloat16)
        grad_q += matmul(key_cols[:, c * rows : (c + 1) * rows], dscores, NN)
        if c == 0:
            dq_stage[...] = grad_q.T.astype(jnp.bfloat16).reshape(dq_stage.shape)
            dst = dq_out.at[:, columns(my_head)]
            for w, j in line:
                send(dq_stage.at[core_at[j], z_at[w]], dst, qp_sem.at[0], line_id(w, j))
            pltpu.make_async_copy(dq_stage.at[core, z], dst, qp_sem.at[0]).start()
        send_part(c, 0, matmul(dscores, query, NN))

    for copy in sent:
        copy.wait_send()
    arrive(dq_out, qp_sem.at[0])
    arrive(parts, p_sem.at[0])


def sum_kernel(dq, parts, dq_out, dk_out, dv_out, dk_buf, dv_buf, store_sem):
    chips, cores = parts.shape[:2]
    stores = [pltpu.make_async_copy(dq, dq_out, store_sem.at[2])]
    stores[0].start()
    for i, (total, out) in enumerate(((dk_buf, dk_out), (dv_buf, dv_out))):
        for j in range(cores):
            summed = parts[0, j, i].astype(jnp.float32)
            for c in range(1, chips):
                summed += parts[c, j, i].astype(jnp.float32)
            total[:, j * HEAD_DIM : (j + 1) * HEAD_DIM] = summed.astype(jnp.bfloat16)
        stores.append(pltpu.make_async_copy(total, out, store_sem.at[i]))
        stores[-1].start()
    for store in stores:
        store.wait()


def body(query_in, key_in, value_in, out_saved, out_grad, span_place):
    ctx_size, head_size = lax.axis_size("ctx"), lax.axis_size("head")
    chips = ctx_size // CORES
    block = key_in.shape[0]
    token_rows, width = query_in.shape
    heads = head_size * CORES
    rows = CORES * block
    low = jnp.bfloat16
    tokens = (CORES, head_size, token_rows, HEAD_DIM)
    message = (token_rows + DELTA_ROWS, HEAD_DIM)
    keys = (chips, CORES, block, HEAD_DIM)
    pieces = (chips, CORES, 2, block, HEAD_DIM)
    dma = pltpu.SemaphoreType.DMA
    copies = 4 * (ctx_size - 1) + 3 * (heads - 1)
    hbm = pl.BlockSpec(memory_space=pltpu.HBM)
    vmem = pl.BlockSpec(memory_space=pltpu.VMEM)
    pairs = CORES * chips * rows * rows
    grads = pl.pallas_call(
        functools.partial(kernel, ctx_size, head_size),
        out_shape=(pltpu.VMEM(query_in.shape, low), pltpu.VMEM(pieces, low)),
        in_specs=[hbm] * 6,
        out_specs=(vmem, vmem),
        scratch_shapes=[
            pltpu.VMEM(tokens, low),
            pltpu.VMEM((CORES, head_size, *message), low),
            pltpu.VMEM(keys, low),
            pltpu.VMEM(keys, low),
            pltpu.VMEM((HEAD_DIM, chips * rows), low),
            pltpu.VMEM((chips, rows, rows), jnp.float32),
            pltpu.VMEM(pieces, low),
            pltpu.VMEM(tokens, low),
            pltpu.VMEM((token_rows, width), low),
            pltpu.VMEM((token_rows, width), low),
            pltpu.VMEM((heads, *message), low),
            pltpu.SMEM(span_place.shape, span_place.dtype),
            dma((copies,)),
            dma((3,)),
            dma((1,)),
            dma((1,)),
            dma((chips,)),
            dma((chips,)),
            dma((1,)),
            dma((1,)),
        ],
        compiler_params=pltpu.CompilerParams(
            collective_id=0, has_side_effects=True, vmem_limit_bytes=GRANT
        ),
        cost_estimate=pl.CostEstimate(
            flops=5 * pairs * HEAD_DIM, bytes_accessed=10 * query_in.size, transcendentals=pairs
        ),
    )(span_place, query_in, key_in, value_in, out_saved, out_grad)
    shapes = (query_in.shape, key_in.shape, value_in.shape)
    return pl.pallas_call(
        sum_kernel,
        out_shape=tuple(jax.ShapeDtypeStruct(shape, low) for shape in shapes),
        in_specs=[vmem] * 2,
        out_specs=(hbm, hbm, hbm),
        scratch_shapes=[
            pltpu.VMEM(key_in.shape, low),
            pltpu.VMEM(value_in.shape, low),
            dma((3,)),
        ],
        compiler_params=pltpu.CompilerParams(vmem_limit_bytes=SMALL_GRANT),
    )(*grads)


def solution(mesh):
    placed = (
        P(("ctx", "head"), None),
        P("ctx", "head"),
        P("ctx", "head"),
        P(("ctx", "head"), None),
        P(("ctx", "head"), None),
        P(),
    )
    return jax.shard_map(
        body,
        mesh=mesh,
        in_specs=placed,
        out_specs=(P(("ctx", "head"), None), P("ctx", "head"), P("ctx", "head")),
        check_vma=False,
    )
```

```python
import functools
import math

import jax
import jax.numpy as jnp
from jax import lax
from jax.experimental import pallas as pl
from jax.experimental.pallas import tpu as pltpu
from jax.sharding import PartitionSpec as P

HEAD_DIM = 128
CORES = 2
DELTA_ROWS = 16
GRANT = 56 * 1024 * 1024
SMALL_GRANT = 8 * 1024 * 1024
MESH = pl.DeviceIdType.MESH
NT = (((1,), (1,)), ((), ()))
NN = (((1,), (0,)), ((), ()))


def matmul(a, b, dims):
    return lax.dot_general(a, b, dims, preferred_element_type=jnp.float32)


def columns(index):
    return pl.ds(pl.multiple_of(index * HEAD_DIM, HEAD_DIM), HEAD_DIM)


def kernel(
    ctx_size, head_size, place_in, query_in, key_in, value_in, saved_in, grad_in,
    dq_out, parts,
    qbuf, tbuf, kbuf, vbuf, key_cols, pbuf, dp_stage, dq_stage,
    own_grad, own_saved, token_src, place,
    send_sem, local_sem, q_sem, t_sem, k_sem, v_sem, p_sem, qp_sem,
):
    chips = ctx_size // CORES
    rows_high = max(chips // 2, 1)
    block = key_in.shape[0]
    token_rows = query_in.shape[0]
    heads = head_size * CORES
    rows = CORES * block
    span = ctx_size * block // place_in.shape[0]
    spans = rows // span
    scale = HEAD_DIM ** -0.5

    me = lax.axis_index("ctx")
    z = lax.axis_index("head")
    core = lax.rem(me, CORES)
    chip = me // CORES
    low, high = lax.rem(chip, 2), chip // 2

    def other_chip(step):
        return lax.rem(high + step // 2, rows_high) * 2 + lax.rem(low + step % 2, 2)

    def other_core(step):
        return lax.rem(core + step, CORES)

    def other_z(step):
        return lax.rem(z + step, head_size)

    chip_at = [other_chip(step) for step in range(chips)]
    core_at = [other_core(step) for step in range(CORES)]
    z_at = [other_z(step) for step in range(head_size)]
    plane = [(c, j) for c in range(chips) for j in range(CORES) if c or j][::-1]
    line = [(w, j) for w in range(head_size) for j in range(CORES) if w or j][::-1]

    def plane_id(c, j):
        return {"ctx": chip_at[c] * CORES + core_at[j], "head": z}

    def line_id(w, j):
        return {"ctx": chip * CORES + core_at[j], "head": z_at[w]}

    barrier = pltpu.get_barrier_semaphore()
    peers = [line_id(w, j) for w, j in line if w] + [plane_id(c, j) for c, j in plane]
    for peer in peers:
        pl.semaphore_signal(barrier, inc=1, device_id=peer, device_id_type=MESH)

    my_head = z * CORES + core
    held = ((grad_in, own_grad), (saved_in, own_saved), (place_in, place))
    loads = [pltpu.make_async_copy(src, dst, local_sem.at[i]) for i, (src, dst) in enumerate(held)]
    for load in loads:
        load.start()
    pltpu.make_async_copy(query_in.at[:, columns(my_head)], qbuf.at[core, z], q_sem.at[0]).start()
    pltpu.make_async_copy(key_in.at[:, columns(core)], kbuf.at[chip, core], k_sem.at[chip]).start()
    pltpu.make_async_copy(value_in.at[:, columns(core)], vbuf.at[chip, core], v_sem.at[chip]).start()

    pl.semaphore_wait(barrier, len(peers))

    sent = []

    def send(src, dst, sem, device):
        copy = pltpu.make_async_remote_copy(
            src_ref=src, dst_ref=dst, send_sem=send_sem.at[len(sent)], recv_sem=sem,
            device_id=device, device_id_type=MESH,
        )
        copy.start()
        sent.append(copy)

    def arrive(dst, sem):
        pltpu.make_async_copy(dst, dst, sem).wait()

    def send_plane(src, dst, sem):
        for c, j in plane:
            send(src.at[:, columns(core_at[j])], dst.at[chip, core], sem.at[chip], plane_id(c, j))

    for w, j in line:
        src = query_in.at[:, columns(z_at[w] * CORES + core_at[j])]
        send(src, qbuf.at[core, z], q_sem.at[0], line_id(w, j))
    send_plane(key_in, kbuf, k_sem)

    for load in loads:
        load.wait()
    product = own_grad[...].astype(jnp.float32) * own_saved[...].astype(jnp.float32)
    coarse = product.astype(jnp.bfloat16)
    fine = (product - coarse.astype(jnp.float32)).astype(jnp.bfloat16)
    shape = (heads, heads * HEAD_DIM)
    member = lax.broadcasted_iota(jnp.int32, shape, 1) // HEAD_DIM == lax.broadcasted_iota(jnp.int32, shape, 0)
    member = jnp.where(member, 1.0, 0.0).astype(jnp.bfloat16)
    delta = matmul(member, jnp.concatenate([coarse] * head_size, axis=0), NT)
    delta += matmul(member, jnp.concatenate([fine] * head_size, axis=0), NT)
    lane_z = lax.broadcasted_iota(jnp.int32, (heads, block), 1) // token_rows
    delta = jnp.where(lane_z == z, delta, 0.0)
    first = delta.astype(jnp.bfloat16).astype(jnp.float32)
    second = (delta - first).astype(jnp.bfloat16).astype(jnp.float32)
    third = delta - first - second
    padding = jnp.zeros((DELTA_ROWS - 3, block), jnp.float32)
    for h in range(heads):
        at = slice(h * HEAD_DIM, (h + 1) * HEAD_DIM)
        token_src[h, :token_rows] = own_grad[:, at]
        split = jnp.concatenate([first[h : h + 1], second[h : h + 1], third[h : h + 1], padding], axis=0)
        token_src[h, token_rows:] = split.astype(jnp.bfloat16)
    pltpu.make_async_copy(token_src.at[my_head], tbuf.at[core, z], t_sem.at[0]).start()

    for w, j in line:
        send(token_src.at[z_at[w] * CORES + core_at[j]], tbuf.at[core, z], t_sem.at[0], line_id(w, j))
    send_plane(value_in, vbuf, v_sem)

    lane = lax.broadcasted_iota(jnp.int32, (1, rows), 1)
    place_row = jnp.zeros((1, rows), jnp.int32)
    for s in range(spans):
        place_row = jnp.where(lane // span == s, place[chip * spans + s], place_row)
    pos_row = place_row * span + lane % span
    within = lax.broadcasted_iota(jnp.int32, (span, rows), 0)

    arrive(qbuf, q_sem.at[0])
    query = qbuf[...].reshape(rows, HEAD_DIM)
    query_cols = query.T

    def chunk(buf, c):
        return buf[chip_at[c]].reshape(rows, HEAD_DIM)

    tops, sums = [], []
    for c in range(chips):
        arrive(kbuf.at[chip_at[c]], k_sem.at[chip_at[c]])
        keys = chunk(kbuf, c)
        key_cols[:, c * rows : (c + 1) * rows] = keys.T
        scores = matmul(keys, query_cols, NN) * (scale * math.log2(math.e))
        pieces = []
        for s in range(spans):
            limit = pos_row - place[chip_at[c] * spans + s] * span
            pieces.append(jnp.where(within <= limit, scores[s * span : (s + 1) * span], -1e30))
        masked = jnp.concatenate(pieces, axis=0)
        top = jnp.max(masked, axis=0, keepdims=True)
        probs = jnp.exp2(masked - top)
        pbuf[c] = probs
        tops.append(top)
        sums.append(jnp.sum(probs, axis=0, keepdims=True))

    best = functools.reduce(jnp.maximum, tops)
    weights = [jnp.exp2(top - best) for top in tops]
    total = functools.reduce(jnp.add, [w * s for w, s in zip(weights, sums)])
    weights = [w / total for w in weights]

    arrive(tbuf, t_sem.at[0])
    grad = tbuf[:, :, :token_rows].reshape(rows, HEAD_DIM)
    delta_row = jnp.concatenate(
        [
            jnp.sum(
                functools.reduce(
                    jnp.add, [tbuf[j, w, token_rows :].astype(jnp.float32) for w in range(head_size)]
                ),
                axis=0, keepdims=True,
            )
            for j in range(CORES)
        ],
        axis=1,
    )

    grad_cols = grad.T

    def send_part(c, kind, total):
        total = total.astype(jnp.bfloat16)
        for j in range(CORES):
            dp_stage[c, j, kind] = total[j * block : (j + 1) * block]
        for j in range(CORES):
            src, dst = dp_stage.at[c, core_at[j], kind], parts.at[chip, core, kind]
            if c or j:
                send(src, dst, p_sem.at[0], plane_id(c, j))
            else:
                pltpu.make_async_copy(src, dst, p_sem.at[0]).start()

    far_first = list(range(chips))[::-1]
    for c in far_first:
        probs = pbuf[c] * weights[c]
        pbuf[c] = probs
        if c:
            send_part(c, 1, matmul(probs.astype(jnp.bfloat16), grad, NN))

    grad_q = jnp.zeros((HEAD_DIM, rows), jnp.float32)
    for c in far_first:
        arrive(vbuf.at[chip_at[c]], v_sem.at[chip_at[c]])
        dprobs = matmul(chunk(vbuf, c), grad_cols, NN)
        dscores = (pbuf[c] * (dprobs - delta_row) * scale).astype(jnp.bfloat16)
        grad_q += matmul(key_cols[:, c * rows : (c + 1) * rows], dscores, NN)
        if c == 0:
            dq_stage[...] = grad_q.T.astype(jnp.bfloat16).reshape(dq_stage.shape)
            dst = dq_out.at[:, columns(my_head)]
            for w, j in line:
                send(dq_stage.at[core_at[j], z_at[w]], dst, qp_sem.at[0], line_id(w, j))
            pltpu.make_async_copy(dq_stage.at[core, z], dst, qp_sem.at[0]).start()
        send_part(c, 0, matmul(dscores, query, NN))
    send_part(0, 1, matmul(pbuf[0].astype(jnp.bfloat16), grad, NN))

    for copy in sent:
        copy.wait_send()
    arrive(dq_out, qp_sem.at[0])
    arrive(parts, p_sem.at[0])


def sum_kernel(dq, parts, dq_out, dk_out, dv_out, dk_buf, dv_buf, store_sem):
    chips, cores = parts.shape[:2]
    stores = [pltpu.make_async_copy(dq, dq_out, store_sem.at[2])]
    stores[0].start()
    for i, (total, out) in enumerate(((dk_buf, dk_out), (dv_buf, dv_out))):
        for j in range(cores):
            summed = parts[0, j, i].astype(jnp.float32)
            for c in range(1, chips):
                summed += parts[c, j, i].astype(jnp.float32)
            total[:, j * HEAD_DIM : (j + 1) * HEAD_DIM] = summed.astype(jnp.bfloat16)
        stores.append(pltpu.make_async_copy(total, out, store_sem.at[i]))
        stores[-1].start()
    for store in stores:
        store.wait()


def body(query_in, key_in, value_in, out_saved, out_grad, span_place):
    ctx_size, head_size = lax.axis_size("ctx"), lax.axis_size("head")
    chips = ctx_size // CORES
    block = key_in.shape[0]
    token_rows, width = query_in.shape
    heads = head_size * CORES
    rows = CORES * block
    low = jnp.bfloat16
    tokens = (CORES, head_size, token_rows, HEAD_DIM)
    message = (token_rows + DELTA_ROWS, HEAD_DIM)
    keys = (chips, CORES, block, HEAD_DIM)
    pieces = (chips, CORES, 2, block, HEAD_DIM)
    dma = pltpu.SemaphoreType.DMA
    copies = 4 * (ctx_size - 1) + 3 * (heads - 1)
    hbm = pl.BlockSpec(memory_space=pltpu.HBM)
    vmem = pl.BlockSpec(memory_space=pltpu.VMEM)
    pairs = CORES * chips * rows * rows
    grads = pl.pallas_call(
        functools.partial(kernel, ctx_size, head_size),
        out_shape=(pltpu.VMEM(query_in.shape, low), pltpu.VMEM(pieces, low)),
        in_specs=[hbm] * 6,
        out_specs=(vmem, vmem),
        scratch_shapes=[
            pltpu.VMEM(tokens, low),
            pltpu.VMEM((CORES, head_size, *message), low),
            pltpu.VMEM(keys, low),
            pltpu.VMEM(keys, low),
            pltpu.VMEM((HEAD_DIM, chips * rows), low),
            pltpu.VMEM((chips, rows, rows), jnp.float32),
            pltpu.VMEM(pieces, low),
            pltpu.VMEM(tokens, low),
            pltpu.VMEM((token_rows, width), low),
            pltpu.VMEM((token_rows, width), low),
            pltpu.VMEM((heads, *message), low),
            pltpu.SMEM(span_place.shape, span_place.dtype),
            dma((copies,)),
            dma((3,)),
            dma((1,)),
            dma((1,)),
            dma((chips,)),
            dma((chips,)),
            dma((1,)),
            dma((1,)),
        ],
        compiler_params=pltpu.CompilerParams(
            collective_id=0, has_side_effects=True, vmem_limit_bytes=GRANT
        ),
        cost_estimate=pl.CostEstimate(
            flops=5 * pairs * HEAD_DIM, bytes_accessed=10 * query_in.size, transcendentals=pairs
        ),
    )(span_place, query_in, key_in, value_in, out_saved, out_grad)
    shapes = (query_in.shape, key_in.shape, value_in.shape)
    return pl.pallas_call(
        sum_kernel,
        out_shape=tuple(jax.ShapeDtypeStruct(shape, low) for shape in shapes),
        in_specs=[vmem] * 2,
        out_specs=(hbm, hbm, hbm),
        scratch_shapes=[
            pltpu.VMEM(key_in.shape, low),
            pltpu.VMEM(value_in.shape, low),
            dma((3,)),
        ],
        compiler_params=pltpu.CompilerParams(vmem_limit_bytes=SMALL_GRANT),
    )(*grads)


def solution(mesh):
    placed = (
        P(("ctx", "head"), None),
        P("ctx", "head"),
        P("ctx", "head"),
        P(("ctx", "head"), None),
        P(("ctx", "head"), None),
        P(),
    )
    return jax.shard_map(
        body,
        mesh=mesh,
        in_specs=placed,
        out_specs=(P(("ctx", "head"), None), P("ctx", "head"), P("ctx", "head")),
        check_vma=False,
    )
```
